128 devices in a mesh: bucket: 8 (over z, y_lo), dom: 16 (over y_hi, x, core).
Axes of the slice: x: 4, y: 4 (y_hi: 2, y_lo: 2; y = y_hi * 2 + y_lo), z: 4, core: 2. Of those that a mesh axis runs over, the one named last changes fastest.
Arguments:
- entity_table: float32 [16, 512, 400], P('bucket', 'dom'), may hold values from -3 to 3
- adagrad_state: float32 [16, 512], P('bucket', 'dom'), may hold values from 0.1 to 10
- relations: float32 [7424, 400], replicated, may hold values from -3 to 3
- roster: int32 [4, 8, 2], replicated, may hold values from 0 to 15, as said below
- edge_triples: int32 [128, 128, 4, 8, 3], P(('bucket', 'dom')), may hold values from 0 to 8191, as said below
- counts: int32 [128, 128, 4], P(('bucket', 'dom')), may hold values from 0 to 8, as said below
- negatives: int32 [4, 8, 16, 16, 512], P(None, 'bucket', 'dom'), may hold values from 0 to 511
Outputs:
- updated_table: float32 [16, 512, 400], P('bucket', 'dom')
- updated_state: float32 [16, 512], P('bucket', 'dom')
The draws below stay inside these ranges and needn't reach their ends.
Inputs may be any that keep to these rules, and one draw needn't show every extreme that they name: In each step every partition 0 to 15 appears exactly once in roster[s]. `edge_triples`: for receiving device w * 16 + j and step s, every head lies in partition roster[s, w, 0] and every tail in partition roster[s, w, 1]; relation ids lie in 0 to 7423, entity ids in 0 to 8191. `counts`: in every step some receiving device gets 8 live slots from every sending device.
All inputs are finite; a program needn't handle non-finite values.
Results may differ from the reference program's by a relative error of at most 0.0003.
Values sent between devices are 32-bit elements; how exact they have to be, the bound alone decides.
No kernel may reach another device: no remote copies, remote signals or barrier semaphores. Data moves between devices by JAX's collectives and lax.ppermute only.
A program may use at most 128 MiB of HBM per device.

```python
import math
import jax
import jax.numpy as jnp
from jax import lax

D = 400
NREL = 7424
EDGE_DEV = 1024
NNEG = 512
STEPS = 4
NPART = 16
PROWS = 512
NCHUNK = 16
N_BUCKET = 8
N_DOM = 16


def make_roster(key):
    keys = jax.random.split(jax.random.fold_in(key, 77), STEPS)
    orders = jax.vmap(lambda k: jax.random.permutation(k, NPART))(keys)
    return orders.astype(jnp.int32).reshape(STEPS, N_BUCKET, 2)


def draw_roster(key, part):
    return make_roster(key)


def draw_edge_triples(key, part):
    plan = make_roster(key)
    key = jax.random.fold_in(key, 2)
    key_head, key_rel, key_tail = jax.random.split(key, 3)
    devices = N_BUCKET * N_DOM
    cap = EDGE_DEV // devices
    worker = jnp.arange(devices, dtype=jnp.int32) // N_DOM
    src_part = jnp.transpose(plan[:, worker, 0], (1, 0))
    dst_part = jnp.transpose(plan[:, worker, 1], (1, 0))
    shape = (devices, devices, STEPS, cap)
    heads = src_part[None, :, :, None] * PROWS + jax.random.randint(key_head, shape, 0, PROWS)
    rels = jax.random.randint(key_rel, shape, 0, NREL)
    tails = dst_part[None, :, :, None] * PROWS + jax.random.randint(key_tail, shape, 0, PROWS)
    return jnp.stack([heads, rels, tails], axis=-1).astype(jnp.int32)


def draw_counts(key, part):
    key = jax.random.fold_in(key, 3)
    key_level, key_hot, key_count = jax.random.split(key, 3)
    devices = N_BUCKET * N_DOM
    cap = EDGE_DEV // devices
    level = jax.random.randint(key_level, (devices, STEPS), 1, cap + 1)
    hot = jax.random.randint(key_hot, (STEPS,), 0, devices)
    is_hot = jnp.arange(devices)[:, None] == hot[None, :]
    level = jnp.where(is_hot, cap, level)
    lowest = jnp.where(is_hot, cap, level // 2)
    values = jax.random.randint(key_count, (devices, devices, STEPS), lowest[None, :, :], level[None, :, :] + 1)
    return values.astype(jnp.int32)


def draw_entity_table(key, part):
    key = jax.random.fold_in(key, 4)
    shape = (NPART, PROWS, D)
    values = 0.3 * jnp.clip(jax.random.normal(key, shape, jnp.float32), -6.0, 6.0)
    return values.astype(jnp.float32)


def draw_relations(key, part):
    key = jax.random.fold_in(key, 5)
    values = jnp.clip(jax.random.normal(key, (NREL, D), jnp.float32), -3.0, 3.0)
    return values.astype(jnp.float32)


def set_ends(values, stream_key, low, high):
    index_at = [jax.random.randint(jax.random.fold_in(stream_key, axis), (), 0, length) for axis, length in enumerate(values.shape)]
    longest = values.shape.index(max(values.shape))
    neighbour = index_at[:longest] + [(index_at[longest] + 1) % values.shape[longest]] + index_at[longest + 1:]
    return values.at[tuple(index_at)].set(low).at[tuple(neighbour)].set(high)


def steps_of(key, dims, pieces, smallest, top_value):
    factor_of, own = 1.0, jax.random.fold_in(key, 6)
    for dim, blocks in pieces:
        heights = jnp.exp(jax.random.uniform(jax.random.fold_in(own, dim), (blocks,), jnp.float32, smallest / len(pieces), top_value / len(pieces)))
        factor_of = factor_of * jnp.repeat(heights, dims[dim] // blocks).reshape([-1 if axis == dim else 1 for axis in range(len(dims))])
    return factor_of


def setup_inputs(seed: int = 0) -> dict:
    splits = jax.random.split(jax.random.key(seed), 8)
    entity_table = draw_entity_table(jax.random.fold_in(splits[7], 71), 0)
    adagrad_state = jnp.clip(jnp.exp(math.log(10.0) - 4.6051702 * jax.random.uniform(splits[1], (NPART, PROWS), jnp.float32) ** steps_of(splits[1], (NPART, PROWS), ((0, 8), (1, 16)), -0.2, 0.2)), 0.1, 10.0)
    relations = draw_relations(jax.random.fold_in(splits[7], 71), 0)
    roster = draw_roster(jax.random.fold_in(splits[7], 71), 0)
    edge_triples = draw_edge_triples(jax.random.fold_in(splits[7], 71), 0)
    counts = draw_counts(jax.random.fold_in(splits[7], 71), 0)
    negatives = set_ends(jax.random.randint(splits[6], (STEPS, N_BUCKET, N_DOM, NCHUNK, NNEG), 0, PROWS), jax.random.fold_in(splits[6], 1), 0, PROWS - 1).astype(jnp.int32)
    return {"entity_table": entity_table, "adagrad_state": adagrad_state, "relations": relations, "roster": roster, "edge_triples": edge_triples, "counts": counts, "negatives": negatives}


cubic_weight = 0.1
learn_rate = 0.05
epsilon = 1e-06

def rotate(left, right):
    half = left.shape[1] // 2
    left_re, left_im = (left[:, :half], left[:, half:])
    right_re, right_im = (right[:, :half], right[:, half:])
    return jnp.concatenate([left_re * right_re - left_im * right_im, left_re * right_im + left_im * right_re], axis=1)

def unrotate(grad, right):
    half = grad.shape[1] // 2
    grad_re, grad_im = (grad[:, :half], grad[:, half:])
    right_re, right_im = (right[:, :half], right[:, half:])
    return jnp.concatenate([grad_re * right_re + grad_im * right_im, grad_im * right_re - grad_re * right_im], axis=1)

def cubic_grad(values):
    half = values.shape[1] // 2
    real_part, imag_part = (values[:, :half], values[:, half:])
    modulus = jnp.sqrt(real_part * real_part + imag_part * imag_part)
    return 3.0 * cubic_weight * jnp.concatenate([modulus * real_part, modulus * imag_part], axis=1)

def contract_rows(left, right):
    return lax.dot_general(left, right, (((0,), (0,)), ((), ())), precision=lax.Precision.HIGHEST)

def worker_grads(part_src, part_dst, relations, triples, valid, negs, src_label, dst_label):
    prows = part_src.shape[0]
    head_local = triples[:, 0] - src_label * prows
    tail_local = triples[:, 2] - dst_label * prows
    head_rows = jnp.take(part_src, head_local, axis=0)
    rel_rows = jnp.take(relations, triples[:, 1], axis=0)
    tail_rows = jnp.take(part_dst, tail_local, axis=0)
    query = rotate(head_rows, rel_rows)
    scores = lax.dot_general(query, part_dst, (((1,), (1,)), ((), ())), precision=lax.Precision.HIGHEST)
    column = jnp.arange(prows, dtype=jnp.int32)
    head_hot = (head_local[:, None] == column[None, :]).astype(jnp.float32)
    tail_hot = (tail_local[:, None] == column[None, :]).astype(jnp.float32)
    nblock = negs.shape[0]
    block_counts = jnp.zeros((nblock, prows), jnp.float32).at[jnp.arange(nblock, dtype=jnp.int32)[:, None], negs].add(1.0)
    weight = (block_counts[:, None, :] + tail_hot.reshape(nblock, -1, prows)).reshape(scores.shape)
    live = weight > 0
    top = lax.optimization_barrier(jnp.max(jnp.where(live, scores, -1e+30), axis=1, keepdims=True))
    terms = weight * jnp.exp(jnp.where(live, scores - top, -1e+30))
    total = lax.optimization_barrier(jnp.sum(terms, axis=1, keepdims=True))
    adjoint = valid[:, None] * (terms / total - tail_hot)
    grad_query = jnp.dot(adjoint, part_dst, precision=lax.Precision.HIGHEST)
    head_total = unrotate(grad_query, rel_rows) + valid[:, None] * cubic_grad(head_rows)
    tail_reg = valid[:, None] * cubic_grad(tail_rows)
    src_grad = contract_rows(head_hot, head_total)
    dst_grad = contract_rows(adjoint, query) + contract_rows(tail_hot, tail_reg)
    return (src_grad, dst_grad)

def adagrad(values, state, grad):
    new_state = state + lax.optimization_barrier(jnp.mean(grad * grad, axis=-1))
    return (values - learn_rate * grad / jnp.sqrt(new_state + epsilon)[..., None], new_state)

def reference(entity_table, adagrad_state, relations, roster, edge_triples, counts, negatives):
    table = entity_table
    state = adagrad_state
    cap = edge_triples.shape[3]
    for step_index in range(STEPS):
        new_table, new_state = (table, state)
        for worker in range(N_BUCKET):
            pair = roster[step_index, worker]
            block = edge_triples[:, worker * N_DOM:(worker + 1) * N_DOM, step_index]
            triples = jnp.transpose(block, (1, 0, 2, 3)).reshape(-1, 3)
            live_counts = jnp.transpose(counts[:, worker * N_DOM:(worker + 1) * N_DOM, step_index], (1, 0))
            valid = (jnp.arange(cap, dtype=jnp.int32)[None, None, :] < live_counts[:, :, None]).astype(jnp.float32).reshape(-1)
            negs = negatives[step_index, worker].reshape(-1, negatives.shape[-1])
            src_grad, dst_grad = worker_grads(table[pair[0]], table[pair[1]], relations, triples, valid, negs, pair[0], pair[1])
            rows_src, state_src = adagrad(table[pair[0]], state[pair[0]], src_grad)
            rows_dst, state_dst = adagrad(table[pair[1]], state[pair[1]], dst_grad)
            new_table = new_table.at[pair[0]].set(rows_src).at[pair[1]].set(rows_dst)
            new_state = new_state.at[pair[0]].set(state_src).at[pair[1]].set(state_dst)
        table, state = (new_table, new_state)
    return (table, state)
```

```python
import jax
import jax.numpy as jnp
from jax import lax
from jax.experimental import pallas as pl
from jax.experimental.pallas import tpu as pltpu
from jax.sharding import PartitionSpec as P

cubic_weight = 0.1
learn_rate = 0.05
epsilon = 1e-06

HALF = 200
LANES = 128
SHARD = 32
PROWS = 512
CHUNK = 256

VMEM = pl.BlockSpec(memory_space=pltpu.VMEM)
SMEM = pl.BlockSpec(memory_space=pltpu.SMEM)


def dom_perms():
    def move(fn):
        return [(j, fn(j)) for j in range(16)]

    def shift(j, d):
        return (j // 8) * 8 + (((j // 2) % 4 + d) % 4) * 2 + j % 2

    return dict(
        axis="dom",
        plus=move(lambda j: shift(j, 1)),
        minus=move(lambda j: shift(j, 3)),
        flip=move(lambda j: j ^ 8),
        core=move(lambda j: j ^ 1),
    )


def bucket_perms():
    def move(fn):
        return [(w, fn(w)) for w in range(8)]

    return dict(
        axis="bucket",
        plus=move(lambda w: (w + 2) % 8),
        minus=move(lambda w: (w + 6) % 8),
        flip=move(lambda w: w ^ 1),
    )


def spread(block, perms):
    def go(v, name):
        return lax.ppermute(v, perms["axis"], perms[name])

    y = go(block, "flip")
    r0, l0 = go(block, "plus"), go(block, "minus")
    r1, l1 = go(y, "plus"), go(y, "minus")
    f0 = go(r0, "plus")
    f1 = go(l1, "minus")
    return [block, y, r0, r1, l0, l1, f0, f1]


def dom_gather(block):
    perms = dom_perms()
    mine = spread(block, perms)
    return mine + [lax.ppermute(v, "dom", perms["core"]) for v in mine]


def dom_reduce(own, other):
    perms = dom_perms()

    def go(v, name):
        return lax.ppermute(v, "dom", perms[name])

    a = [own[p] + go(other[p], "core") for p in range(8)]
    t6, t7 = go(a[6], "plus"), go(a[7], "minus")
    u2, u5 = go(a[2], "minus"), go(a[5], "plus")
    u4, u3 = go(a[4] + t6, "plus"), go(a[3] + t7, "minus")
    b1 = a[1] + u5 + u3
    v = go(b1, "flip")
    return [a[0], u2, u4, v]


RING_PLACE = (0, 2, 3, 1)


def place_dom(rows, me):
    owner = rows // SHARD
    ring = ((owner // 2) % 4 - (me // 2) % 4) % 4
    where_ring = jnp.where(ring == 0, 0, jnp.where(ring == 3, 1, jnp.where(ring == 1, 2, 3)))
    flip = (owner // 8) ^ (me // 8)
    core = (owner % 2) ^ (me % 2)
    return (8 * core + 2 * where_ring + flip) * SHARD + rows % SHARD


def place_bucket(source, me):
    ring = (source // 2 - me // 2) % 4
    where_ring = jnp.where(ring == 0, 0, jnp.where(ring == 3, 1, jnp.where(ring == 1, 2, 3)))
    return 2 * where_ring + ((source % 2) ^ (me % 2))


def lane_index(shape):
    return lax.broadcasted_iota(jnp.int32, shape, 1)


def select_kernel(sel, *refs):
    blocks, (x_ref, st_ref) = refs[:8], refs[8:]
    lane = lane_index((HALF + 8, LANES))
    picked = []
    for q in range(2):
        place, half = sel[2 * q], sel[2 * q + 1]
        got = blocks[0][...]
        for p in range(1, 8):
            got = jnp.where(place == p, blocks[p][...], got)
        picked.append(jnp.where(half == q, got, pltpu.roll(got, 32 if q else 96, 1)))
    out = jnp.where((lane // SHARD) % 2 == 0, picked[0], picked[1])
    x_ref[...] = out[:HALF]
    st_ref[...] = out[HALF:]


def select_blocks(blocks, sel):
    return pl.pallas_call(
        select_kernel,
        out_shape=(
            jax.ShapeDtypeStruct((HALF, LANES), jnp.float32),
            jax.ShapeDtypeStruct((8, LANES), jnp.float32),
        ),
        in_specs=[SMEM] + [VMEM] * 8,
        out_specs=(VMEM, VMEM),
        cost_estimate=pl.CostEstimate(flops=200000, bytes_accessed=1000000, transcendentals=0),
    )(sel, *blocks)


def adagrad_kernel(a_ref, b_ref, c_ref, d_ref, x_ref, st_ref, out_ref):
    grad = (a_ref[...] + b_ref[...]) + (c_ref[...] + d_ref[...])
    total = jnp.sum(grad * grad, axis=0, keepdims=True)
    total = jnp.broadcast_to(total, (8, LANES))
    total = total + pltpu.roll(total, 64, 1)
    state = st_ref[...] + total / (2.0 * HALF)
    scale = learn_rate / jnp.sqrt(state + epsilon)
    out_ref[:HALF] = x_ref[...] - grad * scale[0:1]
    out_ref[HALF:] = state


def adagrad(parts, x, st):
    return pl.pallas_call(
        adagrad_kernel,
        out_shape=jax.ShapeDtypeStruct((HALF + 8, LANES), jnp.float32),
        in_specs=[VMEM] * 6,
        out_specs=VMEM,
        cost_estimate=pl.CostEstimate(flops=200000, bytes_accessed=700000, transcendentals=0),
    )(*parts, x, st)


def split(v):
    high = v.astype(jnp.bfloat16)
    return high, (v - high.astype(jnp.float32)).astype(jnp.bfloat16)


def nn(a, b):
    return lax.dot_general(a, b, (((1,), (0,)), ((), ())), preferred_element_type=jnp.float32)


def nt(a, b):
    return lax.dot_general(a, b, (((1,), (1,)), ((), ())), preferred_element_type=jnp.float32)


def three(fn, a, b):
    return fn(a[0], b[0]) + (fn(a[0], b[1]) + fn(a[1], b[0]))


def step_kernel(*refs):
    blocks = refs[:16]
    heads, tails, valid, rel, weight, own, other = refs[16:23]
    src, dst, sh, sl, dh, dl, th, tl, src_acc, dst_acc, cnt = refs[23:]
    lane = lane_index((HALF, LANES))

    for q, (to, row) in enumerate(((src, 0), (dst, 0), (src, HALF), (dst, HALF))):
        for t in range(4):
            out = None
            for g in range(4):
                piece = blocks[4 * t + g][...]
                if g != q:
                    piece = pltpu.roll(piece, ((g - q) * SHARD) % LANES, 1)
                out = piece if g == 0 else jnp.where(lane >= g * SHARD, piece, out)
            to[row:row + HALF, t * LANES:(t + 1) * LANES] = out

    sh[...], sl[...] = split(src[...])
    dh[...], dl[...] = split(dst[...])
    th[...], tl[...] = split(dst[...].T)
    src_acc[...] = jnp.zeros_like(src_acc)
    dst_acc[...] = jnp.zeros_like(dst_acc)
    cnt[...] = jnp.zeros_like(cnt)

    def chunk(c, carry):
        def row(ref):
            return jnp.concatenate([ref[pl.ds(2 * c, 1), :], ref[pl.ds(2 * c + 1, 1), :]], axis=1)

        column = lax.broadcasted_iota(jnp.int32, (PROWS, CHUNK), 0)
        live_slot = row(valid)
        head_hot = jnp.where(column == row(heads), 1.0, 0.0).astype(jnp.bfloat16)
        tail_hot = jnp.where(column == row(tails), 1.0, 0.0)
        head = nn(sh[...], head_hot) + nn(sl[...], head_hot)
        turn = rel[pl.ds(pl.multiple_of(c * CHUNK, CHUNK), CHUNK), :].T
        h_re, h_im, r_re, r_im = head[:HALF], head[HALF:], turn[:HALF], turn[HALF:]
        query = split(jnp.concatenate([h_re * r_re - h_im * r_im, h_re * r_im + h_im * r_re], axis=0))
        scores = three(nn, (th[...], tl[...]), query)
        base = weight[...]
        amount = jnp.concatenate([base, base], axis=1) + tail_hot
        live = amount > 0
        top = jnp.max(jnp.where(live, scores, -1e30), axis=0, keepdims=True)
        terms = amount * jnp.exp(jnp.where(live, scores - top, -1e30))
        total = jnp.sum(terms, axis=0, keepdims=True)
        adjoint = split(terms * (live_slot / total) - live_slot * tail_hot)
        back = three(nn, (dh[...], dl[...]), adjoint)
        b_re, b_im = back[:HALF], back[HALF:]
        to_head = split(jnp.concatenate([b_re * r_re + b_im * r_im, b_im * r_re - b_re * r_im], axis=0))
        dst_acc[...] += three(nt, query, adjoint)
        src_acc[...] += nt(to_head[0], head_hot) + nt(to_head[1], head_hot)
        flags = jnp.broadcast_to(live_slot, (16, CHUNK)).astype(jnp.bfloat16)
        cnt[0] += nt(flags, head_hot)
        cnt[1] += nt(flags, tail_hot.astype(jnp.bfloat16))
        return carry

    lax.fori_loop(0, 1024 // CHUNK, chunk, 0)

    for i, (rows, acc) in enumerate(((src, src_acc), (dst, dst_acc))):
        re, im = rows[:HALF], rows[HALF:]
        pull = (3.0 * cubic_weight) * jnp.sqrt(re * re + im * im) * cnt[i, 0:1]
        acc[:HALF] += pull * re
        acc[HALF:] += pull * im

    for p in range(16):
        t, g = divmod(p, 4)
        out = None
        for q, (acc, row) in enumerate(((src_acc, 0), (dst_acc, 0), (src_acc, HALF), (dst_acc, HALF))):
            piece = acc[row:row + HALF, t * LANES:(t + 1) * LANES]
            if q != g:
                piece = pltpu.roll(piece, ((q - g) * SHARD) % LANES, 1)
            out = piece if q == 0 else jnp.where(lane >= q * SHARD, piece, out)
        (own if p < 8 else other)[p % 8] = out


def step_grads(blocks, heads, tails, valid, rel, weight):
    f32, bf16 = jnp.float32, jnp.bfloat16
    return pl.pallas_call(
        step_kernel,
        out_shape=(jax.ShapeDtypeStruct((8, HALF, LANES), f32),) * 2,
        in_specs=[VMEM] * 21,
        out_specs=(VMEM, VMEM),
        scratch_shapes=[
            pltpu.VMEM((2 * HALF, PROWS), f32),
            pltpu.VMEM((2 * HALF, PROWS), f32),
            pltpu.VMEM((2 * HALF, PROWS), bf16),
            pltpu.VMEM((2 * HALF, PROWS), bf16),
            pltpu.VMEM((2 * HALF, PROWS), bf16),
            pltpu.VMEM((2 * HALF, PROWS), bf16),
            pltpu.VMEM((PROWS, 2 * HALF), bf16),
            pltpu.VMEM((PROWS, 2 * HALF), bf16),
            pltpu.VMEM((2 * HALF, PROWS), f32),
            pltpu.VMEM((2 * HALF, PROWS), f32),
            pltpu.VMEM((2, 16, PROWS), f32),
        ],
        compiler_params=pltpu.CompilerParams(vmem_limit_bytes=40 * 1024 * 1024),
        cost_estimate=pl.CostEstimate(flops=6_000_000_000, bytes_accessed=6_000_000, transcendentals=600_000),
    )(*blocks, heads, tails, valid, rel, weight)


def locate(labels, wanted, me):
    at = jnp.argmax(labels.reshape(-1)[None, :] == wanted[:, None], axis=1).astype(jnp.int32)
    place = place_bucket(at // 2, me)
    return jnp.stack([place[0], at[0] % 2, place[1], at[1] % 2])


def local(entity_table, adagrad_state, relations, roster, edge_triples, counts, negatives):
    my_bucket = lax.axis_index("bucket")
    my_dom = lax.axis_index("dom")
    steps, cap = edge_triples.shape[2], edge_triples.shape[3]
    devices = edge_triples.shape[1]

    edges = jnp.transpose(edge_triples[0], (1, 3, 2, 0)).reshape(steps * 3 * cap, devices)
    packed = jnp.concatenate(
        [edges, counts[0].T, jnp.zeros((LANES - steps * (3 * cap + 1), devices), jnp.int32)], axis=0
    ).T
    arrived = lax.all_to_all(packed, ("bucket", "dom"), split_axis=0, concat_axis=0, tiled=True).T

    rows = entity_table.reshape(2 * SHARD, 2 * HALF).T
    state = adagrad_state.reshape(1, 2 * SHARD)
    held = jnp.concatenate(
        [
            jnp.concatenate([rows[:HALF], rows[HALF:]], axis=1),
            jnp.broadcast_to(jnp.concatenate([state, state], axis=1), (8, LANES)),
        ],
        axis=0,
    )
    homes = jnp.arange(16, dtype=jnp.int32)
    labels = homes
    column = jnp.arange(PROWS, dtype=jnp.int32)
    for s in range(steps):
        wanted = roster[s, my_bucket]
        x, st = select_blocks(spread(held, bucket_perms()), locate(labels, wanted, my_bucket))
        gathered = dom_gather(x)
        base = s * 3 * cap
        heads = place_dom(arrived[base:base + cap] - wanted[0] * PROWS, my_dom)
        rel = jnp.take(relations, arrived[base + cap:base + 2 * cap].reshape(-1), axis=0, mode="clip")
        tails = place_dom(arrived[base + 2 * cap:base + 3 * cap] - wanted[1] * PROWS, my_dom)
        slot = lax.broadcasted_iota(jnp.int32, (cap, devices), 0)
        valid = (slot < arrived[steps * 3 * cap + s][None, :]).astype(jnp.float32)
        negs = place_dom(negatives[s, 0, 0], my_dom)
        drawn = jnp.sum((negs[:, :, None] == column[None, None, :]).astype(jnp.float32), axis=1)
        weight = jnp.repeat(drawn.T, devices // drawn.shape[0], axis=1)
        own, other = step_grads(gathered, heads, tails, valid, rel, weight)
        held = adagrad(dom_reduce(own, other), x, st)
        labels = roster[s].reshape(-1)
    wanted = 2 * my_bucket + jnp.arange(2, dtype=jnp.int32)
    x, st = select_blocks(spread(held, bucket_perms()), locate(labels, wanted, my_bucket))
    rows = jnp.concatenate([x[:, :64], x[:, 64:]], axis=0).T.reshape(2, SHARD, 2 * HALF)
    return rows, st[0, :64].reshape(2, SHARD)


def solution(mesh):
    in_specs = (
        P("bucket", "dom", None),
        P("bucket", "dom"),
        P(),
        P(),
        P(("bucket", "dom"), None, None, None, None),
        P(("bucket", "dom"), None, None),
        P(None, "bucket", "dom", None, None),
    )
    out_specs = (P("bucket", "dom", None), P("bucket", "dom"))
    return jax.shard_map(local, mesh=mesh, in_specs=in_specs, out_specs=out_specs, check_vma=False)
```

```python
import functools

import jax
import jax.numpy as jnp
from jax import lax
from jax.experimental import pallas as pl
from jax.experimental.pallas import tpu as pltpu
from jax.sharding import PartitionSpec as P

cubic_weight = 0.1
learn_rate = 0.05
epsilon = 1e-06

HALF = 200
LANES = 128
SHARD = 32
PROWS = 512
CHUNK = 256
MIB = 1024 * 1024

VMEM = pl.BlockSpec(memory_space=pltpu.VMEM)
SMEM = pl.BlockSpec(memory_space=pltpu.SMEM)
ANY = pl.BlockSpec(memory_space=pl.ANY)


def dom_perms():
    def move(fn):
        return [(j, fn(j)) for j in range(16)]

    def shift(j, d):
        return (j // 8) * 8 + (((j // 2) % 4 + d) % 4) * 2 + j % 2

    return dict(
        axis="dom",
        plus=move(lambda j: shift(j, 1)),
        minus=move(lambda j: shift(j, 3)),
        flip=move(lambda j: j ^ 8),
        core=move(lambda j: j ^ 1),
    )


def bucket_perms():
    def move(fn):
        return [(w, fn(w)) for w in range(8)]

    return dict(
        axis="bucket",
        plus=move(lambda w: (w + 2) % 8),
        minus=move(lambda w: (w + 6) % 8),
        flip=move(lambda w: w ^ 1),
    )


def tied(value, *extra):
    out = lax.optimization_barrier((value,) + extra)
    return out[0], out[1:]


def spread(block, perms, early=None, late=None):
    def go(v, name):
        return lax.ppermute(v, perms["axis"], perms[name])

    y = go(block, "flip")
    r0, l0 = go(block, "plus"), go(block, "minus")
    if early is not None:
        y, (early,) = tied(y, early)
    r1, l1 = go(y, "plus"), go(y, "minus")
    f0 = go(r0, "plus")
    if late is not None:
        l1, (late,) = tied(l1, late)
    f1 = go(l1, "minus")
    return [block, y, r0, r1, l0, l1, f0, f1], early, late


def dom_gather(block, early=None):
    perms = dom_perms()
    mine, early, _ = spread(block, perms, early)
    return early, mine + [lax.ppermute(v, "dom", perms["core"]) for v in mine]


def dom_reduce(own, other, early=None, late=None):
    perms = dom_perms()

    def go(v, name):
        return lax.ppermute(v, "dom", perms[name])

    swapped = [go(v, "core") for v in other]
    to_plus, to_minus = own[0] + swapped[0], own[1] + swapped[1]
    plus, minus = go(to_plus, "plus"), go(to_minus, "minus")
    on_plus = own[2][0] + swapped[2][0] + plus[0]
    on_minus = own[2][1] + swapped[2][1] + minus[0]
    if early is not None:
        on_plus, (on_minus, early) = tied(on_plus, on_minus, early)
    u4, u3 = go(on_plus, "plus"), go(on_minus, "minus")
    flipped = (own[2][2] + swapped[2][2]) + (plus[1] + u3)
    if late is not None:
        flipped, (late,) = tied(flipped, late)
    return (own[2], swapped[2], minus, u4, go(flipped, "flip")), early, late


SLOTS = {6: (0, 0), 5: (0, 1), 7: (1, 0), 2: (1, 1), 4: (2, 0), 3: (2, 1), 1: (2, 2), 0: (2, 3)}


def ring_place(ring):
    return jnp.where(ring == 0, 0, jnp.where(ring == 3, 1, jnp.where(ring == 1, 2, 3)))


def place_dom(rows, me):
    owner = rows >> 5
    ring = ((owner >> 1) - (me >> 1)) & 3
    flip = ((owner >> 3) ^ (me >> 3)) & 1
    core = (owner ^ me) & 1
    return ((core << 3) + (ring_place(ring) << 1) + flip) * SHARD + (rows & (SHARD - 1))


def place_bucket(source, me):
    return (ring_place(((source >> 1) - (me >> 1)) & 3) << 1) + ((source ^ me) & 1)


def lane_index(shape):
    return lax.broadcasted_iota(jnp.int32, shape, 1)


def select_kernel(exchange, steps, roster, *refs):
    blocks, (x_ref, st_ref) = refs[:8], refs[8:]
    me = lax.axis_index("bucket")
    lane = lane_index((HALF + 8, LANES))
    picked = []
    for q in range(2):
        wanted = 2 * me + q if exchange == steps else roster[exchange, 2 * me + q]
        at = jnp.int32(0)
        for i in range(16):
            label = i if exchange == 0 else roster[exchange - 1, i]
            at = jnp.where(wanted == label, jnp.int32(i), at)
        place, half = place_bucket(at >> 1, me), at & 1
        got = blocks[0][...]
        for p in range(1, 8):
            got = jnp.where(place == p, blocks[p][...], got)
        picked.append(jnp.where(half == q, got, pltpu.roll(got, 32 if q else 96, 1)))
    out = jnp.where((lane // SHARD) % 2 == 0, picked[0], picked[1])
    x_ref[...] = out[:HALF]
    st_ref[...] = out[HALF:]


def select_blocks(blocks, roster, exchange):
    return pl.pallas_call(
        functools.partial(select_kernel, exchange, roster.shape[0]),
        out_shape=(
            jax.ShapeDtypeStruct((HALF, LANES), jnp.float32),
            jax.ShapeDtypeStruct((8, LANES), jnp.float32),
        ),
        in_specs=[SMEM] + [VMEM] * 8,
        out_specs=(VMEM, VMEM),
        compiler_params=pltpu.CompilerParams(vmem_limit_bytes=4 * MIB),
        cost_estimate=pl.CostEstimate(flops=200000, bytes_accessed=500000, transcendentals=0),
    )(roster, *blocks)


def adagrad_kernel(own, swapped, minus, ring, flipped, x_ref, st_ref, out_ref):
    grad = (own[3] + swapped[3]) + ((minus[1] + ring[...]) + flipped[...])
    total = jnp.sum(grad * grad, axis=0, keepdims=True)
    total = jnp.broadcast_to(total, (8, LANES))
    total = total + pltpu.roll(total, 64, 1)
    state = st_ref[...] + total / (2.0 * HALF)
    scale = learn_rate / jnp.sqrt(state + epsilon)
    out_ref[:HALF] = x_ref[...] - grad * scale[0:1]
    out_ref[HALF:] = state


def adagrad(parts, x, st):
    return pl.pallas_call(
        adagrad_kernel,
        out_shape=jax.ShapeDtypeStruct((HALF + 8, LANES), jnp.float32),
        in_specs=[VMEM] * 7,
        out_specs=VMEM,
        compiler_params=pltpu.CompilerParams(vmem_limit_bytes=4 * MIB),
        cost_estimate=pl.CostEstimate(flops=200000, bytes_accessed=700000, transcendentals=0),
    )(*parts, x, st)


def split(v):
    high = v.astype(jnp.bfloat16)
    return high, (v - high.astype(jnp.float32)).astype(jnp.bfloat16)


def nn(a, b):
    return lax.dot_general(a, b, (((1,), (0,)), ((), ())), preferred_element_type=jnp.float32)


def nt(a, b):
    return lax.dot_general(a, b, (((1,), (1,)), ((), ())), preferred_element_type=jnp.float32)


def tn(a, b):
    return lax.dot_general(a, b, (((0,), (0,)), ((), ())), preferred_element_type=jnp.float32)


def three(fn, a, b):
    return fn(a[0], b[0]) + (fn(a[0], b[1]) + fn(a[1], b[0]))


def step_kernel(step, steps, roster, arrived, drawn, *refs):
    blocks, turns, outs, scratch = refs[:16], refs[16], refs[17:23], refs[23:]
    src, dst, sh, sl, dh, dl, th, tl, src_acc, dst_acc, cnt, rel, weight, heads, tails, valid, sem = scratch
    lane = lane_index((HALF, LANES))
    slots = 4 * CHUNK
    fetch = pltpu.make_async_copy(turns, rel, sem)
    fetch.start()

    me = lax.axis_index("bucket")
    dom = lax.axis_index("dom")
    base = step * 24
    heads[...] = place_dom(arrived[base:base + 8] - roster[step, 2 * me] * PROWS, dom)
    tails[...] = place_dom(arrived[base + 16:base + 24] - roster[step, 2 * me + 1] * PROWS, dom)
    slot = lax.broadcasted_iota(jnp.int32, (8, LANES), 0)
    valid[...] = jnp.where(slot < arrived[24 * steps + step:24 * steps + step + 1], 1.0, 0.0)

    for t in range(4):
        for q, (to, row) in enumerate(((src, 0), (dst, 0), (src, HALF), (dst, HALF))):
            out = None
            for g in range(4):
                piece = blocks[4 * t + g][...]
                if g != q:
                    piece = pltpu.roll(piece, ((g - q) * SHARD) % LANES, 1)
                out = piece if g == 0 else jnp.where(lane >= g * SHARD, piece, out)
            to[row:row + HALF, t * LANES:(t + 1) * LANES] = out

    sh[...], sl[...] = split(src[...])
    dh[...], dl[...] = split(dst[...])
    th[...], tl[...] = split(dst[...].T)
    src_acc[...] = jnp.zeros_like(src_acc)
    dst_acc[...] = jnp.zeros_like(dst_acc)
    cnt[...] = jnp.zeros_like(cnt)
    count = split(drawn[...])
    mine = lax.broadcasted_iota(jnp.int32, (16, LANES), 0) == lax.broadcasted_iota(jnp.int32, (16, LANES), 1) // 8
    mine = jnp.where(mine, 1.0, 0.0).astype(jnp.bfloat16)
    weight[...] = tn(count[0], mine) + tn(count[1], mine)
    fetch.wait()

    def chunk(c, carry):
        def row(ref):
            return jnp.concatenate([ref[pl.ds(2 * c, 1), :], ref[pl.ds(2 * c + 1, 1), :]], axis=1)

        column = lax.broadcasted_iota(jnp.int32, (PROWS, CHUNK), 0)
        live_slot = row(valid)
        head_hot = jnp.where(column == row(heads), 1.0, 0.0).astype(jnp.bfloat16)
        tail_hot = jnp.where(column == row(tails), 1.0, 0.0)
        head = nn(sh[...], head_hot) + nn(sl[...], head_hot)
        turn = rel[pl.ds(pl.multiple_of(c * CHUNK, CHUNK), CHUNK), :].T
        h_re, h_im, r_re, r_im = head[:HALF], head[HALF:], turn[:HALF], turn[HALF:]
        query = split(jnp.concatenate([h_re * r_re - h_im * r_im, h_re * r_im + h_im * r_re], axis=0))
        scores = three(nn, (th[...], tl[...]), query)
        base = weight[...]
        amount = jnp.concatenate([base, base], axis=1) + tail_hot
        live = amount > 0
        top = jnp.max(jnp.where(live, scores, -1e30), axis=0, keepdims=True)
        terms = amount * jnp.exp(jnp.where(live, scores - top, -1e30))
        total = jnp.sum(terms, axis=0, keepdims=True)
        adjoint = split(terms * (live_slot / total) - live_slot * tail_hot)
        back = three(nn, (dh[...], dl[...]), adjoint)
        b_re, b_im = back[:HALF], back[HALF:]
        to_head = split(jnp.concatenate([b_re * r_re + b_im * r_im, b_im * r_re - b_re * r_im], axis=0))
        dst_acc[...] += three(nt, query, adjoint)
        src_acc[...] += nt(to_head[0], head_hot) + nt(to_head[1], head_hot)
        flags = jnp.broadcast_to(live_slot, (16, CHUNK)).astype(jnp.bfloat16)
        cnt[0] += nt(flags, head_hot)
        cnt[1] += nt(flags, tail_hot.astype(jnp.bfloat16))
        return carry

    lax.fori_loop(0, 1024 // CHUNK, chunk, 0)

    for i, (rows, acc) in enumerate(((src, src_acc), (dst, dst_acc))):
        re, im = rows[:HALF], rows[HALF:]
        pull = (3.0 * cubic_weight) * jnp.sqrt(re * re + im * im) * cnt[i, 0:1]
        acc[:HALF] += pull * re
        acc[HALF:] += pull * im

    for p in range(16):
        t, g = divmod(p, 4)
        out = None
        for q, (acc, row) in enumerate(((src_acc, 0), (dst_acc, 0), (src_acc, HALF), (dst_acc, HALF))):
            piece = acc[row:row + HALF, t * LANES:(t + 1) * LANES]
            if q != g:
                piece = pltpu.roll(piece, ((q - g) * SHARD) % LANES, 1)
            out = piece if q == 0 else jnp.where(lane >= q * SHARD, piece, out)
        array, place = SLOTS[p % 8]
        outs[array + 3 * (p // 8)][place] = out


def table_kernel(in_ref, out_ref):
    def part(i, carry):
        at = pl.multiple_of(i * LANES, LANES)
        out_ref[pl.ds(at, LANES), :] = in_ref[:, pl.ds(at, LANES)].T
        return carry

    lax.fori_loop(0, out_ref.shape[0] // LANES, part, 0)


def by_rows(columns):
    width, count = columns.shape
    half = count // 2
    return pl.pallas_call(
        table_kernel,
        out_shape=jax.ShapeDtypeStruct((count, width), jnp.float32),
        grid=(2,),
        in_specs=[pl.BlockSpec((width, half), lambda i: (0, i))],
        out_specs=pl.BlockSpec((half, width), lambda i: (i, 0)),
        compiler_params=pltpu.CompilerParams(vmem_limit_bytes=58 * MIB),
        cost_estimate=pl.CostEstimate(flops=0, bytes_accessed=27_000_000, transcendentals=0),
    )(columns)


def step_grads(step, roster, arrived, drawn, blocks, turns):
    f32, bf16 = jnp.float32, jnp.bfloat16
    shapes = tuple(jax.ShapeDtypeStruct((n, HALF, LANES), f32) for n in (2, 2, 4))
    outs = pl.pallas_call(
        functools.partial(step_kernel, step, roster.shape[0]),
        out_shape=shapes * 2,
        in_specs=[SMEM] + [VMEM] * 18 + [ANY],
        out_specs=(VMEM,) * 6,
        scratch_shapes=[
            pltpu.VMEM((2 * HALF, PROWS), f32),
            pltpu.VMEM((2 * HALF, PROWS), f32),
            pltpu.VMEM((2 * HALF, PROWS), bf16),
            pltpu.VMEM((2 * HALF, PROWS), bf16),
            pltpu.VMEM((2 * HALF, PROWS), bf16),
            pltpu.VMEM((2 * HALF, PROWS), bf16),
            pltpu.VMEM((PROWS, 2 * HALF), bf16),
            pltpu.VMEM((PROWS, 2 * HALF), bf16),
            pltpu.VMEM((2 * HALF, PROWS), f32),
            pltpu.VMEM((2 * HALF, PROWS), f32),
            pltpu.VMEM((2, 16, PROWS), f32),
            pltpu.VMEM((4 * CHUNK, 2 * HALF), f32),
            pltpu.VMEM((PROWS, LANES), f32),
            pltpu.VMEM((8, LANES), jnp.int32),
            pltpu.VMEM((8, LANES), jnp.int32),
            pltpu.VMEM((8, LANES), f32),
            pltpu.SemaphoreType.DMA,
        ],
        compiler_params=pltpu.CompilerParams(vmem_limit_bytes=20 * MIB),
        cost_estimate=pl.CostEstimate(flops=6_000_000_000, bytes_accessed=6_000_000, transcendentals=600_000),
    )(roster, arrived, drawn, *blocks, turns)
    return outs[:3], outs[3:]


def local(entity_table, adagrad_state, relations, roster, edge_triples, counts, negatives):
    my_dom = lax.axis_index("dom")
    steps, cap = edge_triples.shape[2], edge_triples.shape[3]
    devices = edge_triples.shape[1]

    edges = jnp.transpose(edge_triples[0], (1, 3, 2, 0)).reshape(steps * 3 * cap, devices)
    packed = jnp.concatenate(
        [edges, counts[0].T, jnp.zeros((LANES - steps * (3 * cap + 1), devices), jnp.int32)], axis=0
    ).T
    arrived = lax.all_to_all(packed, ("bucket", "dom"), split_axis=0, concat_axis=0, tiled=True).T

    rows = entity_table.reshape(2 * SHARD, 2 * HALF).T
    state = adagrad_state.reshape(1, 2 * SHARD)
    held = jnp.concatenate(
        [
            jnp.concatenate([rows[:HALF], rows[HALF:]], axis=1),
            jnp.broadcast_to(jnp.concatenate([state, state], axis=1), (8, LANES)),
        ],
        axis=0,
    )
    column = jnp.arange(PROWS, dtype=jnp.int32)
    roster = roster.reshape(steps, 16)

    def drawn(s):
        negs = place_dom(negatives[s, 0, 0], my_dom)
        return jnp.sum((negs[:, :, None] == column[None, None, :]).astype(jnp.float32), axis=1)

    def turns(s):
        base = s * 3 * cap + cap
        return jnp.take(table, arrived[base:base + cap].reshape(-1), axis=0, mode="clip")

    arrived, (table,) = tied(arrived, by_rows(relations.T))
    brought, now_drawn, arrived = spread(held, bucket_perms(), drawn(0), arrived)
    now_turns = turns(0)
    for s in range(steps):
        x, st = select_blocks(brought, roster, s)
        now_turns, gathered = dom_gather(x, now_turns)
        own, other = step_grads(s, roster, arrived, now_drawn, gathered, now_turns)
        more = s + 1 < steps
        parts, now_turns, _ = dom_reduce(own, other, turns(s + 1) if more else None)
        held = adagrad(parts, x, st)
        brought, now_drawn, _ = spread(held, bucket_perms(), drawn(s + 1) if more else None)
    x, st = select_blocks(brought, roster, steps)
    rows = jnp.concatenate([x[:, :64], x[:, 64:]], axis=0).T.reshape(2, SHARD, 2 * HALF)
    return rows, st[0, :64].reshape(2, SHARD)


def solution(mesh):
    in_specs = (
        P("bucket", "dom", None),
        P("bucket", "dom"),
        P(),
        P(),
        P(("bucket", "dom"), None, None, None, None),
        P(("bucket", "dom"), None, None),
        P(None, "bucket", "dom", None, None),
    )
    out_specs = (P("bucket", "dom", None), P("bucket", "dom"))
    return jax.shard_map(local, mesh=mesh, in_specs=in_specs, out_specs=out_specs, check_vma=False)
```

```python
import functools

import jax
import jax.numpy as jnp
from jax import lax
from jax.experimental import pallas as pl
from jax.experimental.pallas import tpu as pltpu
from jax.sharding import PartitionSpec as P

cubic_weight = 0.1
learn_rate = 0.05
epsilon = 1e-06

HALF = 200
LANES = 128
SHARD = 32
PROWS = 512
SLOTS = 1024
MIB = 1024 * 1024

VMEM = pl.BlockSpec(memory_space=pltpu.VMEM)
SMEM = pl.BlockSpec(memory_space=pltpu.SMEM)


def dom_perms():
    def move(fn):
        return [(j, fn(j)) for j in range(16)]

    def shift(j, d):
        return (j // 8) * 8 + (((j // 2) % 4 + d) % 4) * 2 + j % 2

    return dict(
        axis="dom",
        plus=move(lambda j: shift(j, 1)),
        minus=move(lambda j: shift(j, 3)),
        flip=move(lambda j: j ^ 8),
        core=move(lambda j: j ^ 1),
    )


def bucket_perms():
    def move(fn):
        return [(w, fn(w)) for w in range(8)]

    return dict(
        axis="bucket",
        plus=move(lambda w: (w + 2) % 8),
        minus=move(lambda w: (w + 6) % 8),
        flip=move(lambda w: w ^ 1),
    )


def tied(value, *extra):
    out = lax.optimization_barrier((value,) + extra)
    return out[0], out[1:]


def spread(block, perms, early=None, late=None):
    def go(v, name):
        return lax.ppermute(v, perms["axis"], perms[name])

    y = go(block, "flip")
    r0, l0 = go(block, "plus"), go(block, "minus")
    if early is not None:
        y, (early,) = tied(y, early)
    r1, l1 = go(y, "plus"), go(y, "minus")
    f0 = go(r0, "plus")
    if late is not None:
        l1, (late,) = tied(l1, late)
    f1 = go(l1, "minus")
    return [block, y, r0, r1, l0, l1, f0, f1], early, late


def dom_gather(block, early=None):
    perms = dom_perms()
    mine, early, _ = spread(block, perms, early)
    return early, mine + [lax.ppermute(v, "dom", perms["core"]) for v in mine]


def dom_reduce(own, other, early=None, late=None):
    perms = dom_perms()

    def go(v, name):
        return lax.ppermute(v, "dom", perms[name])

    swapped = [go(v, "core") for v in other]
    to_plus, to_minus = own[0] + swapped[0], own[1] + swapped[1]
    plus, minus = go(to_plus, "plus"), go(to_minus, "minus")
    on_plus = own[2][0] + swapped[2][0] + plus[0]
    on_minus = own[2][1] + swapped[2][1] + minus[0]
    if early is not None:
        on_plus, (on_minus, early) = tied(on_plus, on_minus, early)
    u4, u3 = go(on_plus, "plus"), go(on_minus, "minus")
    flipped = (own[2][2] + swapped[2][2]) + (plus[1] + u3)
    if late is not None:
        flipped, (late,) = tied(flipped, late)
    return (own[2], swapped[2], minus, u4, go(flipped, "flip")), early, late


OUT_PLACE = {6: (0, 0), 5: (0, 1), 7: (1, 0), 2: (1, 1), 4: (2, 0), 3: (2, 1), 1: (2, 2), 0: (2, 3)}


def ring_place(ring):
    return jnp.where(ring == 0, 0, jnp.where(ring == 3, 1, jnp.where(ring == 1, 2, 3)))


def place_dom(rows, me):
    owner = rows >> 5
    ring = ((owner >> 1) - (me >> 1)) & 3
    flip = ((owner >> 3) ^ (me >> 3)) & 1
    core = (owner ^ me) & 1
    return ((core << 3) + (ring_place(ring) << 1) + flip) * SHARD + (rows & (SHARD - 1))


def place_bucket(source, me):
    return (ring_place(((source >> 1) - (me >> 1)) & 3) << 1) + ((source ^ me) & 1)


def lane_index(shape):
    return lax.broadcasted_iota(jnp.int32, shape, 1)


def select_kernel(exchange, steps, roster, *refs):
    blocks, (x_ref, st_ref) = refs[:8], refs[8:]
    me = lax.axis_index("bucket")
    lane = lane_index((HALF + 8, LANES))
    picked = []
    for q in range(2):
        wanted = 2 * me + q if exchange == steps else roster[exchange, 2 * me + q]
        at = jnp.int32(0)
        for i in range(16):
            label = i if exchange == 0 else roster[exchange - 1, i]
            at = jnp.where(wanted == label, jnp.int32(i), at)
        place, half = place_bucket(at >> 1, me), at & 1
        got = blocks[0][...]
        for p in range(1, 8):
            got = jnp.where(place == p, blocks[p][...], got)
        picked.append(jnp.where(half == q, got, pltpu.roll(got, 32 if q else 96, 1)))
    out = jnp.where((lane // SHARD) % 2 == 0, picked[0], picked[1])
    x_ref[...] = out[:HALF]
    st_ref[...] = out[HALF:]


def select_blocks(blocks, roster, exchange):
    return pl.pallas_call(
        functools.partial(select_kernel, exchange, roster.shape[0]),
        out_shape=(
            jax.ShapeDtypeStruct((HALF, LANES), jnp.float32),
            jax.ShapeDtypeStruct((8, LANES), jnp.float32),
        ),
        in_specs=[SMEM] + [VMEM] * 8,
        out_specs=(VMEM, VMEM),
        compiler_params=pltpu.CompilerParams(vmem_limit_bytes=4 * MIB),
        cost_estimate=pl.CostEstimate(flops=200000, bytes_accessed=500000, transcendentals=0),
    )(roster, *blocks)


def adagrad_kernel(own, swapped, minus, ring, flipped, x_ref, st_ref, out_ref):
    grad = (own[3] + swapped[3]) + ((minus[1] + ring[...]) + flipped[...])
    total = jnp.sum(grad * grad, axis=0, keepdims=True)
    total = jnp.broadcast_to(total, (8, LANES))
    total = total + pltpu.roll(total, 64, 1)
    state = st_ref[...] + total / (2.0 * HALF)
    scale = learn_rate / jnp.sqrt(state + epsilon)
    out_ref[:HALF] = x_ref[...] - grad * scale[0:1]
    out_ref[HALF:] = state


def adagrad(parts, x, st):
    return pl.pallas_call(
        adagrad_kernel,
        out_shape=jax.ShapeDtypeStruct((HALF + 8, LANES), jnp.float32),
        in_specs=[VMEM] * 7,
        out_specs=VMEM,
        compiler_params=pltpu.CompilerParams(vmem_limit_bytes=4 * MIB),
        cost_estimate=pl.CostEstimate(flops=200000, bytes_accessed=700000, transcendentals=0),
    )(*parts, x, st)


def split(v):
    high = v.astype(jnp.bfloat16)
    return high, (v - high.astype(jnp.float32)).astype(jnp.bfloat16)


def nn(a, b):
    return lax.dot_general(a, b, (((1,), (0,)), ((), ())), preferred_element_type=jnp.float32)


def nt(a, b):
    return lax.dot_general(a, b, (((1,), (1,)), ((), ())), preferred_element_type=jnp.float32)


def tn(a, b):
    return lax.dot_general(a, b, (((0,), (0,)), ((), ())), preferred_element_type=jnp.float32)


def three(fn, a, b):
    return fn(a[0], b[0]) + (fn(a[0], b[1]) + fn(a[1], b[0]))


def exchange_lanes(tiles):
    lane = lane_index((HALF, LANES))
    low, even = lane < 2 * SHARD, (lane // SHARD) % 2 == 0
    a, b, c, d = tiles
    a, c = jnp.where(low, a, pltpu.roll(c, 64, 1)), jnp.where(low, pltpu.roll(a, 64, 1), c)
    b, d = jnp.where(low, b, pltpu.roll(d, 64, 1)), jnp.where(low, pltpu.roll(b, 64, 1), d)
    a, b = jnp.where(even, a, pltpu.roll(b, 32, 1)), jnp.where(even, pltpu.roll(a, 96, 1), b)
    c, d = jnp.where(even, c, pltpu.roll(d, 32, 1)), jnp.where(even, pltpu.roll(c, 96, 1), d)
    return a, b, c, d


def step_kernel(step, steps, roster, arrived, drawn, *refs):
    blocks, rel, outs, scratch = refs[:16], refs[16], refs[17:23], refs[23:]
    src, dst, sh, sl, dh, dl, th, tl = scratch
    me = lax.axis_index("bucket")
    dom = lax.axis_index("dom")
    base = step * 24

    def row(v):
        return jnp.concatenate([v[i:i + 1] for i in range(8)], axis=1)

    heads = row(place_dom(arrived[base:base + 8] - roster[step, 2 * me] * PROWS, dom))
    tails = row(place_dom(arrived[base + 16:base + 24] - roster[step, 2 * me + 1] * PROWS, dom))
    slot = lax.broadcasted_iota(jnp.int32, (8, LANES), 0)
    live_slot = row(jnp.where(slot < arrived[24 * steps + step:24 * steps + step + 1], 1.0, 0.0))

    quarters = ((src, 0), (dst, 0), (src, HALF), (dst, HALF))
    for t in range(4):
        tiles = exchange_lanes([blocks[4 * t + g][...] for g in range(4)])
        for (to, at), tile in zip(quarters, tiles):
            to[at:at + HALF, t * LANES:(t + 1) * LANES] = tile

    sh[...], sl[...] = split(src[...])
    dh[...], dl[...] = split(dst[...])
    th[...], tl[...] = split(dst[...].T)
    count = split(drawn[...])
    mine = lax.broadcasted_iota(jnp.int32, (16, LANES), 0) == lax.broadcasted_iota(jnp.int32, (16, LANES), 1) // 8
    mine = jnp.where(mine, 1.0, 0.0).astype(jnp.bfloat16)
    weight = tn(count[0], mine) + tn(count[1], mine)

    column = lax.broadcasted_iota(jnp.int32, (PROWS, SLOTS), 0)
    head_hot = jnp.where(column == heads, 1.0, 0.0).astype(jnp.bfloat16)
    tail_hot = jnp.where(column == tails, 1.0, 0.0)
    head = nn(sh[...], head_hot) + nn(sl[...], head_hot)
    turn = rel[...].T
    h_re, h_im, r_re, r_im = head[:HALF], head[HALF:], turn[:HALF], turn[HALF:]
    query = split(jnp.concatenate([h_re * r_re - h_im * r_im, h_re * r_im + h_im * r_re], axis=0))
    scores = three(nn, (th[...], tl[...]), query)
    amount = jnp.concatenate([weight] * 8, axis=1) + tail_hot
    scores = jnp.where(amount > 0, scores, -1e30)
    top = jnp.max(scores, axis=0, keepdims=True)
    terms = amount * jnp.exp(scores - top)
    total = jnp.sum(terms, axis=0, keepdims=True)
    adjoint = split(terms * (live_slot / total) - live_slot * tail_hot)
    dst_grad = three(nt, query, adjoint)
    back = three(nn, (dh[...], dl[...]), adjoint)
    b_re, b_im = back[:HALF], back[HALF:]
    to_head = split(jnp.concatenate([b_re * r_re + b_im * r_im, b_im * r_re - b_re * r_im], axis=0))
    src_grad = nt(to_head[0], head_hot) + nt(to_head[1], head_hot)
    flags = jnp.broadcast_to(live_slot, (16, SLOTS)).astype(jnp.bfloat16)
    head_count = nt(flags, head_hot)[0:1]
    tail_count = nt(flags, tail_hot.astype(jnp.bfloat16))[0:1]

    grads = []
    for rows, grad, times in ((src, src_grad, head_count), (dst, dst_grad, tail_count)):
        re, im = rows[:HALF], rows[HALF:]
        modulus = jnp.sqrt(re * re + im * im)
        pull = modulus * ((3.0 * cubic_weight) * times)
        grads.append((grad[:HALF] + pull * re, grad[HALF:] + pull * im))

    for t in range(4):
        at = slice(t * LANES, (t + 1) * LANES)
        tiles = exchange_lanes([grads[0][0][:, at], grads[1][0][:, at], grads[0][1][:, at], grads[1][1][:, at]])
        for g, tile in enumerate(tiles):
            p = 4 * t + g
            array, place = OUT_PLACE[p % 8]
            outs[array + 3 * (p // 8)][place] = tile


def table_kernel(columns, out_ref, came, goes, came_sems, goes_sems):
    depth, out_depth, width = came.shape[0], goes.shape[0], came.shape[2]
    parts = out_ref.shape[0] // width

    def fetch(i):
        at, slot = pl.multiple_of(i * width, width), lax.rem(i, depth)
        return pltpu.make_async_copy(columns.at[:, pl.ds(at, width)], came.at[slot], came_sems.at[slot])

    def store(i):
        at, slot = pl.multiple_of(i * width, width), lax.rem(i, out_depth)
        return pltpu.make_async_copy(goes.at[slot], out_ref.at[pl.ds(at, width), :], goes_sems.at[slot])

    for i in range(depth):
        fetch(jnp.int32(i)).start()

    def part(i, carry):
        fetch(i).wait()

        @pl.when(i >= out_depth)
        def _():
            store(i - out_depth).wait()

        goes[lax.rem(i, out_depth)] = came[lax.rem(i, depth)].T
        store(i).start()

        @pl.when(i + depth < parts)
        def _():
            fetch(i + depth).start()

        return carry

    lax.fori_loop(0, parts, part, 0)
    for i in range(parts - out_depth, parts):
        store(jnp.int32(i)).wait()


def by_rows(columns):
    width, count = columns.shape
    part = 2 * LANES
    return pl.pallas_call(
        table_kernel,
        out_shape=jax.ShapeDtypeStruct((count, width), jnp.float32),
        in_specs=[pl.BlockSpec(memory_space=pl.ANY)],
        out_specs=pl.BlockSpec(memory_space=pl.ANY),
        scratch_shapes=[
            pltpu.VMEM((8, width, part), jnp.float32),
            pltpu.VMEM((4, part, width), jnp.float32),
            pltpu.SemaphoreType.DMA((8,)),
            pltpu.SemaphoreType.DMA((4,)),
        ],
        compiler_params=pltpu.CompilerParams(vmem_limit_bytes=58 * MIB),
        cost_estimate=pl.CostEstimate(flops=0, bytes_accessed=27_000_000, transcendentals=0),
    )(columns)


def turns_kernel(ids, table, out_ref):
    def group(c, carry):
        rows = [table[pl.ds(ids[c // 8, (c % 8) * 16 + u], 1), :] for u in range(16)]
        for u, row in enumerate(rows):
            out_ref[pl.ds(c * 16 + u, 1), :] = row
        return carry

    lax.fori_loop(0, SLOTS // 16, group, 0)


def fetch_turns(table, ids):
    return pl.pallas_call(
        turns_kernel,
        out_shape=jax.ShapeDtypeStruct((SLOTS, table.shape[1]), jnp.float32),
        in_specs=[SMEM, VMEM],
        out_specs=VMEM,
        compiler_params=pltpu.CompilerParams(vmem_limit_bytes=4 * MIB),
        cost_estimate=pl.CostEstimate(flops=0, bytes_accessed=20_000_000, transcendentals=0),
    )(ids, table)


def step_grads(step, roster, arrived, drawn, blocks, turns):
    f32, bf16 = jnp.float32, jnp.bfloat16
    shapes = tuple(jax.ShapeDtypeStruct((n, HALF, LANES), f32) for n in (2, 2, 4))
    outs = pl.pallas_call(
        functools.partial(step_kernel, step, roster.shape[0]),
        out_shape=shapes * 2,
        in_specs=[SMEM] + [VMEM] * 19,
        out_specs=(VMEM,) * 6,
        scratch_shapes=[
            pltpu.VMEM((2 * HALF, PROWS), f32),
            pltpu.VMEM((2 * HALF, PROWS), f32),
            pltpu.VMEM((2 * HALF, PROWS), bf16),
            pltpu.VMEM((2 * HALF, PROWS), bf16),
            pltpu.VMEM((2 * HALF, PROWS), bf16),
            pltpu.VMEM((2 * HALF, PROWS), bf16),
            pltpu.VMEM((PROWS, 2 * HALF), bf16),
            pltpu.VMEM((PROWS, 2 * HALF), bf16),
        ],
        compiler_params=pltpu.CompilerParams(vmem_limit_bytes=20 * MIB),
        cost_estimate=pl.CostEstimate(flops=6_000_000_000, bytes_accessed=6_000_000, transcendentals=600_000),
    )(roster, arrived, drawn, *blocks, turns)
    return outs[:3], outs[3:]


def local(entity_table, adagrad_state, relations, roster, edge_triples, counts, negatives):
    my_dom = lax.axis_index("dom")
    steps, cap = edge_triples.shape[2], edge_triples.shape[3]
    devices = edge_triples.shape[1]

    edges = jnp.transpose(edge_triples[0], (1, 3, 2, 0)).reshape(steps * 3 * cap, devices)
    packed = jnp.concatenate(
        [edges, counts[0].T, jnp.zeros((LANES - steps * (3 * cap + 1), devices), jnp.int32)], axis=0
    ).T
    arrived = lax.all_to_all(packed, ("bucket", "dom"), split_axis=0, concat_axis=0, tiled=True).T

    rows = entity_table.reshape(2 * SHARD, 2 * HALF).T
    state = adagrad_state.reshape(1, 2 * SHARD)
    held = jnp.concatenate(
        [
            jnp.concatenate([rows[:HALF], rows[HALF:]], axis=1),
            jnp.broadcast_to(jnp.concatenate([state, state], axis=1), (8, LANES)),
        ],
        axis=0,
    )
    column = jnp.arange(PROWS, dtype=jnp.int32)
    roster = roster.reshape(steps, 16)

    def drawn(s):
        negs = place_dom(negatives[s, 0, 0], my_dom)
        return jnp.sum((negs[:, :, None] == column[None, None, :]).astype(jnp.float32), axis=1)

    def turns(s):
        base = s * 3 * cap + cap
        return fetch_turns(table, arrived[base:base + cap])

    arrived, (table,) = tied(arrived, by_rows(relations.T))
    brought, now_drawn, arrived = spread(held, bucket_perms(), drawn(0), arrived)
    now_turns = turns(0)
    for s in range(steps):
        x, st = select_blocks(brought, roster, s)
        now_turns, gathered = dom_gather(x, now_turns)
        own, other = step_grads(s, roster, arrived, now_drawn, gathered, now_turns)
        more = s + 1 < steps
        parts, now_turns, _ = dom_reduce(own, other, turns(s + 1) if more else None)
        held = adagrad(parts, x, st)
        brought, now_drawn, _ = spread(held, bucket_perms(), drawn(s + 1) if more else None)
    x, st = select_blocks(brought, roster, steps)
    rows = jnp.concatenate([x[:, :64], x[:, 64:]], axis=0).T.reshape(2, SHARD, 2 * HALF)
    return rows, st[0, :64].reshape(2, SHARD)


def solution(mesh):
    in_specs = (
        P("bucket", "dom", None),
        P("bucket", "dom"),
        P(),
        P(),
        P(("bucket", "dom"), None, None, None, None),
        P(("bucket", "dom"), None, None),
        P(None, "bucket", "dom", None, None),
    )
    out_specs = (P("bucket", "dom", None), P("bucket", "dom"))
    return jax.shard_map(local, mesh=mesh, in_specs=in_specs, out_specs=out_specs, check_vma=False)
```

```python
import functools

import jax
import jax.numpy as jnp
from jax import lax
from jax.experimental import pallas as pl
from jax.experimental.pallas import tpu as pltpu
from jax.sharding import PartitionSpec as P

cubic_weight = 0.1
learn_rate = 0.05
epsilon = 1e-06

HALF = 200
LANES = 128
SHARD = 32
PROWS = 512
SLOTS = 1024
MIB = 1024 * 1024

VMEM = pl.BlockSpec(memory_space=pltpu.VMEM)
SMEM = pl.BlockSpec(memory_space=pltpu.SMEM)


def dom_perms():
    def move(fn):
        return [(j, fn(j)) for j in range(16)]

    def shift(j, d):
        return (j // 8) * 8 + (((j // 2) % 4 + d) % 4) * 2 + j % 2

    return dict(
        axis="dom",
        plus=move(lambda j: shift(j, 1)),
        minus=move(lambda j: shift(j, 3)),
        far=move(lambda j: shift(j, 2)),
        flip=move(lambda j: j ^ 8),
        core=move(lambda j: j ^ 1),
    )


def bucket_perms():
    def move(fn):
        return [(w, fn(w)) for w in range(8)]

    return dict(
        axis="bucket",
        plus=move(lambda w: (w + 2) % 8),
        minus=move(lambda w: (w + 6) % 8),
        far=move(lambda w: (w + 4) % 8),
        flip=move(lambda w: w ^ 1),
    )


def tied(value, *extra):
    out = lax.optimization_barrier((value,) + extra)
    return out[0], out[1:]


def spread(block, perms, early=None, late=None):
    def go(v, name):
        return lax.ppermute(v, perms["axis"], perms[name])

    y = go(block, "flip")
    if early is not None:
        y, (early,) = tied(y, early)
    both = jnp.concatenate([block, y], axis=0)
    r, l, f = go(both, "plus"), go(both, "minus"), go(both, "far")
    if late is not None:
        f, (late,) = tied(f, late)
    return [both, r, l, f], early, late


def dom_gather(block, early=None):
    perms = dom_perms()
    mine, early, _ = spread(block, perms, early)
    return early, mine + [lax.ppermute(v, "dom", perms["core"]) for v in mine]


def dom_reduce(own, other, early=None, late=None):
    perms = dom_perms()

    def go(v, name):
        return lax.ppermute(v, "dom", perms[name])

    swapped = [go(v, "core") for v in other]
    to_plus, to_minus = own[0] + swapped[0], own[1] + swapped[1]
    plus, minus = go(to_plus, "plus"), go(to_minus, "minus")
    on_plus = own[2][0] + swapped[2][0] + plus[0]
    on_minus = own[2][1] + swapped[2][1] + minus[0]
    if early is not None:
        on_plus, (on_minus, early) = tied(on_plus, on_minus, early)
    u4, u3 = go(on_plus, "plus"), go(on_minus, "minus")
    flipped = (own[2][2] + swapped[2][2]) + (plus[1] + u3)
    if late is not None:
        flipped, (late,) = tied(flipped, late)
    return (own[2], swapped[2], minus, u4, go(flipped, "flip")), early, late


OUT_PLACE = {6: (0, 0), 5: (0, 1), 7: (1, 0), 2: (1, 1), 4: (2, 0), 3: (2, 1), 1: (2, 2), 0: (2, 3)}


def ring_place(ring):
    return jnp.where(ring == 0, 0, jnp.where(ring == 3, 1, jnp.where(ring == 1, 2, 3)))


def place_dom(rows, me):
    owner = rows >> 5
    ring = ((owner >> 1) - (me >> 1)) & 3
    flip = ((owner >> 3) ^ (me >> 3)) & 1
    core = (owner ^ me) & 1
    return ((core << 3) + (ring_place(ring) << 1) + flip) * SHARD + (rows & (SHARD - 1))


def place_bucket(source, me):
    return (ring_place(((source >> 1) - (me >> 1)) & 3) << 1) + ((source ^ me) & 1)


def lane_index(shape):
    return lax.broadcasted_iota(jnp.int32, shape, 1)


def views(arrays, rows):
    return [(ref, at) for ref in arrays for at in range(0, ref.shape[0], rows)]


def read(ref, at, rows):
    return ref[at:at + rows]


def select_kernel(exchange, steps, roster, *refs):
    blocks, (x_ref, st_ref) = views(refs[:-2], HALF + 8), refs[-2:]
    me = lax.axis_index("bucket")
    lane = lane_index((HALF + 8, LANES))
    picked = []
    for q in range(2):
        wanted = 2 * me + q if exchange == steps else roster[exchange, 2 * me + q]
        at = jnp.int32(0)
        for i in range(16):
            label = i if exchange == 0 else roster[exchange - 1, i]
            at = jnp.where(wanted == label, jnp.int32(i), at)
        place, half = place_bucket(at >> 1, me), at & 1
        got = read(*blocks[0], HALF + 8)
        for p in range(1, 8):
            got = jnp.where(place == p, read(*blocks[p], HALF + 8), got)
        picked.append(jnp.where(half == q, got, pltpu.roll(got, 32 if q else 96, 1)))
    out = jnp.where((lane // SHARD) % 2 == 0, picked[0], picked[1])
    x_ref[...] = out[:HALF]
    st_ref[...] = out[HALF:]


def select_blocks(blocks, roster, exchange):
    return pl.pallas_call(
        functools.partial(select_kernel, exchange, roster.shape[0]),
        out_shape=(
            jax.ShapeDtypeStruct((HALF, LANES), jnp.float32),
            jax.ShapeDtypeStruct((8, LANES), jnp.float32),
        ),
        in_specs=[SMEM] + [VMEM] * len(blocks),
        out_specs=(VMEM, VMEM),
        compiler_params=pltpu.CompilerParams(vmem_limit_bytes=4 * MIB),
        cost_estimate=pl.CostEstimate(flops=200000, bytes_accessed=500000, transcendentals=0),
    )(roster, *blocks)


def adagrad_kernel(own, swapped, minus, ring, flipped, x_ref, st_ref, out_ref):
    grad = (own[3] + swapped[3]) + ((minus[1] + ring[...]) + flipped[...])
    total = jnp.sum(grad * grad, axis=0, keepdims=True)
    total = jnp.broadcast_to(total, (8, LANES))
    total = total + pltpu.roll(total, 64, 1)
    state = st_ref[...] + total / (2.0 * HALF)
    scale = learn_rate / jnp.sqrt(state + epsilon)
    out_ref[:HALF] = x_ref[...] - grad * scale[0:1]
    out_ref[HALF:] = state


def adagrad(parts, x, st):
    return pl.pallas_call(
        adagrad_kernel,
        out_shape=jax.ShapeDtypeStruct((HALF + 8, LANES), jnp.float32),
        in_specs=[VMEM] * 7,
        out_specs=VMEM,
        compiler_params=pltpu.CompilerParams(vmem_limit_bytes=4 * MIB),
        cost_estimate=pl.CostEstimate(flops=200000, bytes_accessed=700000, transcendentals=0),
    )(*parts, x, st)


def split(v):
    high = v.astype(jnp.bfloat16)
    return high, (v - high.astype(jnp.float32)).astype(jnp.bfloat16)


def nn(a, b):
    return lax.dot_general(a, b, (((1,), (0,)), ((), ())), preferred_element_type=jnp.float32)


def nt(a, b):
    return lax.dot_general(a, b, (((1,), (1,)), ((), ())), preferred_element_type=jnp.float32)


def tn(a, b):
    return lax.dot_general(a, b, (((0,), (0,)), ((), ())), preferred_element_type=jnp.float32)


def three(fn, a, b):
    return fn(a[0], b[0]) + (fn(a[0], b[1]) + fn(a[1], b[0]))


def exchange_lanes(tiles):
    lane = lane_index((HALF, LANES))
    low, even = lane < 2 * SHARD, (lane // SHARD) % 2 == 0
    a, b, c, d = tiles
    a, c = jnp.where(low, a, pltpu.roll(c, 64, 1)), jnp.where(low, pltpu.roll(a, 64, 1), c)
    b, d = jnp.where(low, b, pltpu.roll(d, 64, 1)), jnp.where(low, pltpu.roll(b, 64, 1), d)
    a, b = jnp.where(even, a, pltpu.roll(b, 32, 1)), jnp.where(even, pltpu.roll(a, 96, 1), b)
    c, d = jnp.where(even, c, pltpu.roll(d, 32, 1)), jnp.where(even, pltpu.roll(c, 96, 1), d)
    return a, b, c, d


def step_kernel(step, steps, roster, arrived, drawn, *refs):
    arrays, rel, outs, scratch = refs[:-15], refs[-15], refs[-14:-8], refs[-8:]
    blocks = views(arrays, HALF)
    src, dst, sh, sl, dh, dl, th, tl = scratch
    me = lax.axis_index("bucket")
    dom = lax.axis_index("dom")
    base = step * 24

    def row(v):
        return jnp.concatenate([v[i:i + 1] for i in range(8)], axis=1)

    heads = row(place_dom(arrived[base:base + 8] - roster[step, 2 * me] * PROWS, dom))
    tails = row(place_dom(arrived[base + 16:base + 24] - roster[step, 2 * me + 1] * PROWS, dom))
    slot = lax.broadcasted_iota(jnp.int32, (8, LANES), 0)
    live_slot = row(jnp.where(slot < arrived[24 * steps + step:24 * steps + step + 1], 1.0, 0.0))

    quarters = ((src, 0), (dst, 0), (src, HALF), (dst, HALF))
    for t in range(4):
        tiles = exchange_lanes([read(*blocks[4 * t + g], HALF) for g in range(4)])
        for (to, at), tile in zip(quarters, tiles):
            to[at:at + HALF, t * LANES:(t + 1) * LANES] = tile

    sh[...], sl[...] = split(src[...])
    dh[...], dl[...] = split(dst[...])
    th[...], tl[...] = split(dst[...].T)
    count = split(drawn[...])
    mine = lax.broadcasted_iota(jnp.int32, (16, LANES), 0) == lax.broadcasted_iota(jnp.int32, (16, LANES), 1) // 8
    mine = jnp.where(mine, 1.0, 0.0).astype(jnp.bfloat16)
    weight = tn(count[0], mine) + tn(count[1], mine)

    column = lax.broadcasted_iota(jnp.int32, (PROWS, SLOTS), 0)
    head_hot = jnp.where(column == heads, 1.0, 0.0).astype(jnp.bfloat16)
    tail_hot = jnp.where(column == tails, 1.0, 0.0)
    head = nn(sh[...], head_hot) + nn(sl[...], head_hot)
    turn = rel[...].T
    h_re, h_im, r_re, r_im = head[:HALF], head[HALF:], turn[:HALF], turn[HALF:]
    query = split(jnp.concatenate([h_re * r_re - h_im * r_im, h_re * r_im + h_im * r_re], axis=0))
    scores = three(nn, (th[...], tl[...]), query)
    amount = jnp.concatenate([weight] * 8, axis=1) + tail_hot
    scores = jnp.where(amount > 0, scores, -1e30)
    top = jnp.max(scores, axis=0, keepdims=True)
    terms = amount * jnp.exp(scores - top)
    total = jnp.sum(terms, axis=0, keepdims=True)
    adjoint = split(terms * (live_slot / total) - live_slot * tail_hot)
    dst_grad = three(nt, query, adjoint)
    back = three(nn, (dh[...], dl[...]), adjoint)
    b_re, b_im = back[:HALF], back[HALF:]
    to_head = split(jnp.concatenate([b_re * r_re + b_im * r_im, b_im * r_re - b_re * r_im], axis=0))
    src_grad = nt(to_head[0], head_hot) + nt(to_head[1], head_hot)
    flags = jnp.broadcast_to(live_slot, (16, SLOTS)).astype(jnp.bfloat16)
    head_count = nt(flags, head_hot)[0:1]
    tail_count = nt(flags, tail_hot.astype(jnp.bfloat16))[0:1]

    grads = []
    for rows, grad, times in ((src, src_grad, head_count), (dst, dst_grad, tail_count)):
        re, im = rows[:HALF], rows[HALF:]
        modulus = jnp.sqrt(re * re + im * im)
        pull = modulus * ((3.0 * cubic_weight) * times)
        grads.append((grad[:HALF] + pull * re, grad[HALF:] + pull * im))

    for t in range(4):
        at = slice(t * LANES, (t + 1) * LANES)
        tiles = exchange_lanes([grads[0][0][:, at], grads[1][0][:, at], grads[0][1][:, at], grads[1][1][:, at]])
        for g, tile in enumerate(tiles):
            p = 4 * t + g
            array, place = OUT_PLACE[p % 8]
            outs[array + 3 * (p // 8)][place] = tile


def table_kernel(columns, out_ref, came, goes, came_sems, goes_sems):
    depth, out_depth, width = came.shape[0], goes.shape[0], came.shape[2]
    parts = out_ref.shape[0] // width

    def fetch(i):
        at, slot = pl.multiple_of(i * width, width), lax.rem(i, depth)
        return pltpu.make_async_copy(columns.at[:, pl.ds(at, width)], came.at[slot], came_sems.at[slot])

    def store(i):
        at, slot = pl.multiple_of(i * width, width), lax.rem(i, out_depth)
        return pltpu.make_async_copy(goes.at[slot], out_ref.at[pl.ds(at, width), :], goes_sems.at[slot])

    for i in range(depth):
        fetch(jnp.int32(i)).start()

    def part(i, carry):
        fetch(i).wait()

        @pl.when(i >= out_depth)
        def _():
            store(i - out_depth).wait()

        goes[lax.rem(i, out_depth)] = came[lax.rem(i, depth)].T
        store(i).start()

        @pl.when(i + depth < parts)
        def _():
            fetch(i + depth).start()

        return carry

    lax.fori_loop(0, parts, part, 0)
    for i in range(parts - out_depth, parts):
        store(jnp.int32(i)).wait()


def by_rows(columns):
    width, count = columns.shape
    part = 2 * LANES
    return pl.pallas_call(
        table_kernel,
        out_shape=jax.ShapeDtypeStruct((count, width), jnp.float32),
        in_specs=[pl.BlockSpec(memory_space=pl.ANY)],
        out_specs=pl.BlockSpec(memory_space=pl.ANY),
        scratch_shapes=[
            pltpu.VMEM((8, width, part), jnp.float32),
            pltpu.VMEM((4, part, width), jnp.float32),
            pltpu.SemaphoreType.DMA((8,)),
            pltpu.SemaphoreType.DMA((4,)),
        ],
        compiler_params=pltpu.CompilerParams(vmem_limit_bytes=58 * MIB),
        cost_estimate=pl.CostEstimate(flops=0, bytes_accessed=27_000_000, transcendentals=0),
    )(columns)


def turns_kernel(ids, table, out_ref):
    def group(c, carry):
        rows = [table[pl.ds(ids[c // 8, (c % 8) * 16 + u], 1), :] for u in range(16)]
        for u, row in enumerate(rows):
            out_ref[pl.ds(c * 16 + u, 1), :] = row
        return carry

    lax.fori_loop(0, SLOTS // 16, group, 0)


def fetch_turns(table, ids):
    return pl.pallas_call(
        turns_kernel,
        out_shape=jax.ShapeDtypeStruct((SLOTS, table.shape[1]), jnp.float32),
        in_specs=[SMEM, VMEM],
        out_specs=VMEM,
        compiler_params=pltpu.CompilerParams(vmem_limit_bytes=4 * MIB),
        cost_estimate=pl.CostEstimate(flops=0, bytes_accessed=20_000_000, transcendentals=0),
    )(ids, table)


def step_grads(step, roster, arrived, drawn, blocks, turns):
    f32, bf16 = jnp.float32, jnp.bfloat16
    shapes = tuple(jax.ShapeDtypeStruct((n, HALF, LANES), f32) for n in (2, 2, 4))
    outs = pl.pallas_call(
        functools.partial(step_kernel, step, roster.shape[0]),
        out_shape=shapes * 2,
        in_specs=[SMEM] + [VMEM] * (3 + len(blocks)),
        out_specs=(VMEM,) * 6,
        scratch_shapes=[
            pltpu.VMEM((2 * HALF, PROWS), f32),
            pltpu.VMEM((2 * HALF, PROWS), f32),
            pltpu.VMEM((2 * HALF, PROWS), bf16),
            pltpu.VMEM((2 * HALF, PROWS), bf16),
            pltpu.VMEM((2 * HALF, PROWS), bf16),
            pltpu.VMEM((2 * HALF, PROWS), bf16),
            pltpu.VMEM((PROWS, 2 * HALF), bf16),
            pltpu.VMEM((PROWS, 2 * HALF), bf16),
        ],
        compiler_params=pltpu.CompilerParams(vmem_limit_bytes=20 * MIB),
        cost_estimate=pl.CostEstimate(flops=6_000_000_000, bytes_accessed=6_000_000, transcendentals=600_000),
    )(roster, arrived, drawn, *blocks, turns)
    return outs[:3], outs[3:]


def local(entity_table, adagrad_state, relations, roster, edge_triples, counts, negatives):
    my_dom = lax.axis_index("dom")
    steps, cap = edge_triples.shape[2], edge_triples.shape[3]
    devices = edge_triples.shape[1]

    edges = jnp.transpose(edge_triples[0], (1, 3, 2, 0)).reshape(steps * 3 * cap, devices)
    packed = jnp.concatenate(
        [edges, counts[0].T, jnp.zeros((LANES - steps * (3 * cap + 1), devices), jnp.int32)], axis=0
    ).T
    arrived = lax.all_to_all(packed, ("bucket", "dom"), split_axis=0, concat_axis=0, tiled=True).T

    rows = entity_table.reshape(2 * SHARD, 2 * HALF).T
    state = adagrad_state.reshape(1, 2 * SHARD)
    held = jnp.concatenate(
        [
            jnp.concatenate([rows[:HALF], rows[HALF:]], axis=1),
            jnp.broadcast_to(jnp.concatenate([state, state], axis=1), (8, LANES)),
        ],
        axis=0,
    )
    column = jnp.arange(PROWS, dtype=jnp.int32)
    roster = roster.reshape(steps, 16)

    def drawn(s):
        negs = place_dom(negatives[s, 0, 0], my_dom)
        return jnp.sum((negs[:, :, None] == column[None, None, :]).astype(jnp.float32), axis=1)

    def turns(s):
        base = s * 3 * cap + cap
        return fetch_turns(table, arrived[base:base + cap])

    arrived, (table,) = tied(arrived, by_rows(relations.T))
    brought, now_drawn, arrived = spread(held, bucket_perms(), drawn(0), arrived)
    now_turns = turns(0)
    for s in range(steps):
        x, st = select_blocks(brought, roster, s)
        now_turns, gathered = dom_gather(x, now_turns)
        own, other = step_grads(s, roster, arrived, now_drawn, gathered, now_turns)
        more = s + 1 < steps
        parts, now_turns, _ = dom_reduce(own, other, turns(s + 1) if more else None)
        held = adagrad(parts, x, st)
        brought, now_drawn, _ = spread(held, bucket_perms(), drawn(s + 1) if more else None)
    x, st = select_blocks(brought, roster, steps)
    rows = jnp.concatenate([x[:, :64], x[:, 64:]], axis=0).T.reshape(2, SHARD, 2 * HALF)
    return rows, st[0, :64].reshape(2, SHARD)


def solution(mesh):
    in_specs = (
        P("bucket", "dom", None),
        P("bucket", "dom"),
        P(),
        P(),
        P(("bucket", "dom"), None, None, None, None),
        P(("bucket", "dom"), None, None),
        P(None, "bucket", "dom", None, None),
    )
    out_specs = (P("bucket", "dom", None), P("bucket", "dom"))
    return jax.shard_map(local, mesh=mesh, in_specs=in_specs, out_specs=out_specs, check_vma=False)
```

```python
import functools

import jax
import jax.numpy as jnp
from jax import lax
from jax.experimental import pallas as pl
from jax.experimental.pallas import tpu as pltpu
from jax.sharding import PartitionSpec as P

cubic_weight = 0.1
learn_rate = 0.05
epsilon = 1e-06

HALF = 200
LANES = 128
SHARD = 32
PROWS = 512
SLOTS = 1024
MIB = 1024 * 1024

VMEM = pl.BlockSpec(memory_space=pltpu.VMEM)
SMEM = pl.BlockSpec(memory_space=pltpu.SMEM)


def dom_perms():
    def move(fn):
        return [(j, fn(j)) for j in range(16)]

    def shift(j, d):
        return (j // 8) * 8 + (((j // 2) % 4 + d) % 4) * 2 + j % 2

    return dict(
        axis="dom",
        plus=move(lambda j: shift(j, 1)),
        minus=move(lambda j: shift(j, 3)),
        far=move(lambda j: shift(j, 2)),
        flip=move(lambda j: j ^ 8),
        core=move(lambda j: j ^ 1),
    )


def bucket_perms():
    def move(fn):
        return [(w, fn(w)) for w in range(8)]

    return dict(
        axis="bucket",
        plus=move(lambda w: (w + 2) % 8),
        minus=move(lambda w: (w + 6) % 8),
        far=move(lambda w: (w + 4) % 8),
        flip=move(lambda w: w ^ 1),
    )


def tied(value, *extra):
    out = lax.optimization_barrier((value,) + extra)
    return out[0], out[1:]


def spread(block, perms, early=None, late=None):
    def go(v, name):
        return lax.ppermute(v, perms["axis"], perms[name])

    y = go(block, "flip")
    if early is not None:
        y, (early,) = tied(y, early)
    both = jnp.concatenate([block, y], axis=0)
    r, l, f = go(both, "plus"), go(both, "minus"), go(both, "far")
    if late is not None:
        f, (late,) = tied(f, late)
    return [both, r, l, f], early, late


def dom_gather(block, early=None, late=None):
    perms = dom_perms()
    mine, early, late = spread(block, perms, early, late)
    return early, late, mine + [lax.ppermute(v, "dom", perms["core"]) for v in mine]


def dom_reduce(own, other, early=None, late=None):
    perms = dom_perms()

    def go(v, name):
        return lax.ppermute(v, "dom", perms[name])

    swapped = [go(v, "core") for v in other]
    to_plus, to_minus = own[0] + swapped[0], own[1] + swapped[1]
    plus, minus = go(to_plus, "plus"), go(to_minus, "minus")
    on_plus = own[2][0] + swapped[2][0] + plus[0]
    on_minus = own[2][1] + swapped[2][1] + minus[0]
    if early is not None:
        on_plus, (on_minus, early) = tied(on_plus, on_minus, early)
    u4, u3 = go(on_plus, "plus"), go(on_minus, "minus")
    flipped = (own[2][2] + swapped[2][2]) + (plus[1] + u3)
    if late is not None:
        flipped, (late,) = tied(flipped, late)
    return (own[2], swapped[2], minus, u4, go(flipped, "flip")), early, late


OUT_PLACE = {6: (0, 0), 5: (0, 1), 7: (1, 0), 2: (1, 1), 4: (2, 0), 3: (2, 1), 1: (2, 2), 0: (2, 3)}


def ring_place(ring):
    return jnp.where(ring == 0, 0, jnp.where(ring == 3, 1, jnp.where(ring == 1, 2, 3)))


def place_dom(rows, me):
    owner = rows >> 5
    ring = ((owner >> 1) - (me >> 1)) & 3
    flip = ((owner >> 3) ^ (me >> 3)) & 1
    core = (owner ^ me) & 1
    return ((core << 3) + (ring_place(ring) << 1) + flip) * SHARD + (rows & (SHARD - 1))


def place_bucket(source, me):
    return (ring_place(((source >> 1) - (me >> 1)) & 3) << 1) + ((source ^ me) & 1)


def lane_index(shape):
    return lax.broadcasted_iota(jnp.int32, shape, 1)


def views(arrays, rows):
    return [(ref, at) for ref in arrays for at in range(0, ref.shape[0], rows)]


def read(ref, at, rows):
    return ref[at:at + rows]


def select_kernel(exchange, steps, roster, *refs):
    blocks, (x_ref, st_ref) = views(refs[:-2], HALF + 8), refs[-2:]
    me = lax.axis_index("bucket")
    lane = lane_index((HALF + 8, LANES))
    picked = []
    for q in range(2):
        wanted = 2 * me + q if exchange == steps else roster[exchange, 2 * me + q]
        at = jnp.int32(0)
        for i in range(16):
            label = i if exchange == 0 else roster[exchange - 1, i]
            at = jnp.where(wanted == label, jnp.int32(i), at)
        place, half = place_bucket(at >> 1, me), at & 1
        got = read(*blocks[0], HALF + 8)
        for p in range(1, 8):
            got = jnp.where(place == p, read(*blocks[p], HALF + 8), got)
        picked.append(jnp.where(half == q, got, pltpu.roll(got, 32 if q else 96, 1)))
    out = jnp.where((lane // SHARD) % 2 == 0, picked[0], picked[1])
    x_ref[...] = out[:HALF]
    st_ref[...] = out[HALF:]


def select_blocks(blocks, roster, exchange):
    return pl.pallas_call(
        functools.partial(select_kernel, exchange, roster.shape[0]),
        out_shape=(
            jax.ShapeDtypeStruct((HALF, LANES), jnp.float32),
            jax.ShapeDtypeStruct((8, LANES), jnp.float32),
        ),
        in_specs=[SMEM] + [VMEM] * len(blocks),
        out_specs=(VMEM, VMEM),
        compiler_params=pltpu.CompilerParams(vmem_limit_bytes=4 * MIB),
        cost_estimate=pl.CostEstimate(flops=200000, bytes_accessed=500000, transcendentals=0),
    )(roster, *blocks)


def adagrad_kernel(own, swapped, minus, ring, flipped, x_ref, st_ref, out_ref):
    grad = (own[3] + swapped[3]) + ((minus[1] + ring[...]) + flipped[...])
    total = jnp.sum(grad * grad, axis=0, keepdims=True)
    total = jnp.broadcast_to(total, (8, LANES))
    total = total + pltpu.roll(total, 64, 1)
    state = st_ref[...] + total / (2.0 * HALF)
    scale = learn_rate / jnp.sqrt(state + epsilon)
    out_ref[:HALF] = x_ref[...] - grad * scale[0:1]
    out_ref[HALF:] = state


def adagrad(parts, x, st):
    return pl.pallas_call(
        adagrad_kernel,
        out_shape=jax.ShapeDtypeStruct((HALF + 8, LANES), jnp.float32),
        in_specs=[VMEM] * 7,
        out_specs=VMEM,
        compiler_params=pltpu.CompilerParams(vmem_limit_bytes=4 * MIB),
        cost_estimate=pl.CostEstimate(flops=200000, bytes_accessed=700000, transcendentals=0),
    )(*parts, x, st)


def split(v):
    high = v.astype(jnp.bfloat16)
    return high, (v - high.astype(jnp.float32)).astype(jnp.bfloat16)


def nn(a, b):
    return lax.dot_general(a, b, (((1,), (0,)), ((), ())), preferred_element_type=jnp.float32)


def nt(a, b):
    return lax.dot_general(a, b, (((1,), (1,)), ((), ())), preferred_element_type=jnp.float32)


def tn(a, b):
    return lax.dot_general(a, b, (((0,), (0,)), ((), ())), preferred_element_type=jnp.float32)


def three(fn, a, b):
    return fn(a[0], b[0]) + (fn(a[0], b[1]) + fn(a[1], b[0]))


def exchange_lanes(tiles):
    lane = lane_index((HALF, LANES))
    low, even = lane < 2 * SHARD, (lane // SHARD) % 2 == 0
    a, b, c, d = tiles
    a, c = jnp.where(low, a, pltpu.roll(c, 64, 1)), jnp.where(low, pltpu.roll(a, 64, 1), c)
    b, d = jnp.where(low, b, pltpu.roll(d, 64, 1)), jnp.where(low, pltpu.roll(b, 64, 1), d)
    a, b = jnp.where(even, a, pltpu.roll(b, 32, 1)), jnp.where(even, pltpu.roll(a, 96, 1), b)
    c, d = jnp.where(even, c, pltpu.roll(d, 32, 1)), jnp.where(even, pltpu.roll(c, 96, 1), d)
    return a, b, c, d


def step_kernel(step, steps, roster, arrived, drawn, *refs):
    arrays, rel, outs, scratch = refs[:-15], refs[-15], refs[-14:-8], refs[-8:]
    blocks = views(arrays, HALF)
    src, dst, sh, sl, dh, dl, th, tl = scratch
    me = lax.axis_index("bucket")
    dom = lax.axis_index("dom")
    base = step * 24

    def row(v):
        return jnp.concatenate([v[i:i + 1] for i in range(8)], axis=1)

    heads = row(place_dom(arrived[base:base + 8] - roster[step, 2 * me] * PROWS, dom))
    tails = row(place_dom(arrived[base + 16:base + 24] - roster[step, 2 * me + 1] * PROWS, dom))
    slot = lax.broadcasted_iota(jnp.int32, (8, LANES), 0)
    live_slot = row(jnp.where(slot < arrived[24 * steps + step:24 * steps + step + 1], 1.0, 0.0))

    quarters = ((src, 0), (dst, 0), (src, HALF), (dst, HALF))
    for t in range(4):
        tiles = exchange_lanes([read(*blocks[4 * t + g], HALF) for g in range(4)])
        for (to, at), tile in zip(quarters, tiles):
            to[at:at + HALF, t * LANES:(t + 1) * LANES] = tile

    sh[...], sl[...] = split(src[...])
    dh[...], dl[...] = split(dst[...])
    th[...], tl[...] = split(dst[...].T)
    count = split(drawn[...])
    mine = lax.broadcasted_iota(jnp.int32, (16, LANES), 0) == lax.broadcasted_iota(jnp.int32, (16, LANES), 1) // 8
    mine = jnp.where(mine, 1.0, 0.0).astype(jnp.bfloat16)
    weight = tn(count[0], mine) + tn(count[1], mine)

    column = lax.broadcasted_iota(jnp.int32, (PROWS, SLOTS), 0)
    head_hot = jnp.where(column == heads, 1.0, 0.0).astype(jnp.bfloat16)
    tail_hot = jnp.where(column == tails, 1.0, 0.0)
    head = nn(sh[...], head_hot) + nn(sl[...], head_hot)
    turn = rel[...].T
    h_re, h_im, r_re, r_im = head[:HALF], head[HALF:], turn[:HALF], turn[HALF:]
    query = split(jnp.concatenate([h_re * r_re - h_im * r_im, h_re * r_im + h_im * r_re], axis=0))
    scores = three(nn, (th[...], tl[...]), query)
    amount = jnp.concatenate([weight] * 8, axis=1) + tail_hot
    scores = jnp.where(amount > 0, scores, -1e30)
    top = jnp.max(scores, axis=0, keepdims=True)
    terms = amount * jnp.exp(scores - top)
    total = jnp.sum(terms, axis=0, keepdims=True)
    adjoint = split(terms * (live_slot / total) - live_slot * tail_hot)
    dst_grad = three(nt, query, adjoint)
    back = three(nn, (dh[...], dl[...]), adjoint)
    b_re, b_im = back[:HALF], back[HALF:]
    to_head = split(jnp.concatenate([b_re * r_re + b_im * r_im, b_im * r_re - b_re * r_im], axis=0))
    src_grad = nt(to_head[0], head_hot) + nt(to_head[1], head_hot)
    flags = jnp.broadcast_to(live_slot, (16, SLOTS)).astype(jnp.bfloat16)
    head_count = nt(flags, head_hot)[0:1]
    tail_count = nt(flags, tail_hot.astype(jnp.bfloat16))[0:1]

    grads = []
    for rows, grad, times in ((src, src_grad, head_count), (dst, dst_grad, tail_count)):
        re, im = rows[:HALF], rows[HALF:]
        modulus = jnp.sqrt(re * re + im * im)
        pull = modulus * ((3.0 * cubic_weight) * times)
        grads.append((grad[:HALF] + pull * re, grad[HALF:] + pull * im))

    for t in range(4):
        at = slice(t * LANES, (t + 1) * LANES)
        tiles = exchange_lanes([grads[0][0][:, at], grads[1][0][:, at], grads[0][1][:, at], grads[1][1][:, at]])
        for g, tile in enumerate(tiles):
            p = 4 * t + g
            array, place = OUT_PLACE[p % 8]
            outs[array + 3 * (p // 8)][place] = tile


def table_kernel(columns, out_ref, came, goes, came_sems, goes_sems):
    depth, out_depth, width = came.shape[0], goes.shape[0], came.shape[2]
    parts = out_ref.shape[0] // width

    def fetch(i):
        at, slot = pl.multiple_of(i * width, width), lax.rem(i, depth)
        return pltpu.make_async_copy(columns.at[:, pl.ds(at, width)], came.at[slot], came_sems.at[slot])

    def store(i):
        at, slot = pl.multiple_of(i * width, width), lax.rem(i, out_depth)
        return pltpu.make_async_copy(goes.at[slot], out_ref.at[pl.ds(at, width), :], goes_sems.at[slot])

    for i in range(depth):
        fetch(jnp.int32(i)).start()

    def part(i, carry):
        fetch(i).wait()

        @pl.when(i >= out_depth)
        def _():
            store(i - out_depth).wait()

        goes[lax.rem(i, out_depth)] = came[lax.rem(i, depth)].T
        store(i).start()

        @pl.when(i + depth < parts)
        def _():
            fetch(i + depth).start()

        return carry

    lax.fori_loop(0, parts, part, 0)
    for i in range(parts - out_depth, parts):
        store(jnp.int32(i)).wait()


def by_rows(columns):
    width, count = columns.shape
    part = 2 * LANES
    return pl.pallas_call(
        table_kernel,
        out_shape=jax.ShapeDtypeStruct((count, width), jnp.float32),
        in_specs=[pl.BlockSpec(memory_space=pl.ANY)],
        out_specs=pl.BlockSpec(memory_space=pl.ANY),
        scratch_shapes=[
            pltpu.VMEM((8, width, part), jnp.float32),
            pltpu.VMEM((4, part, width), jnp.float32),
            pltpu.SemaphoreType.DMA((8,)),
            pltpu.SemaphoreType.DMA((4,)),
        ],
        compiler_params=pltpu.CompilerParams(vmem_limit_bytes=58 * MIB),
        cost_estimate=pl.CostEstimate(flops=0, bytes_accessed=27_000_000, transcendentals=0),
    )(columns)


def turns_kernel(ids, table, out_ref):
    def group(c, carry):
        rows = [table[pl.ds(ids[c // 8, (c % 8) * 16 + u], 1), :] for u in range(16)]
        for u, row in enumerate(rows):
            out_ref[pl.ds(c * 16 + u, 1), :] = row
        return carry

    lax.fori_loop(0, SLOTS // 16, group, 0)


def fetch_turns(table, ids):
    return pl.pallas_call(
        turns_kernel,
        out_shape=jax.ShapeDtypeStruct((SLOTS, table.shape[1]), jnp.float32),
        in_specs=[SMEM, VMEM],
        out_specs=VMEM,
        compiler_params=pltpu.CompilerParams(vmem_limit_bytes=4 * MIB),
        cost_estimate=pl.CostEstimate(flops=0, bytes_accessed=20_000_000, transcendentals=0),
    )(ids, table)


def step_grads(step, roster, arrived, drawn, blocks, turns):
    f32, bf16 = jnp.float32, jnp.bfloat16
    shapes = tuple(jax.ShapeDtypeStruct((n, HALF, LANES), f32) for n in (2, 2, 4))
    outs = pl.pallas_call(
        functools.partial(step_kernel, step, roster.shape[0]),
        out_shape=shapes * 2,
        in_specs=[SMEM] + [VMEM] * (3 + len(blocks)),
        out_specs=(VMEM,) * 6,
        scratch_shapes=[
            pltpu.VMEM((2 * HALF, PROWS), f32),
            pltpu.VMEM((2 * HALF, PROWS), f32),
            pltpu.VMEM((2 * HALF, PROWS), bf16),
            pltpu.VMEM((2 * HALF, PROWS), bf16),
            pltpu.VMEM((2 * HALF, PROWS), bf16),
            pltpu.VMEM((2 * HALF, PROWS), bf16),
            pltpu.VMEM((PROWS, 2 * HALF), bf16),
            pltpu.VMEM((PROWS, 2 * HALF), bf16),
        ],
        compiler_params=pltpu.CompilerParams(vmem_limit_bytes=20 * MIB),
        cost_estimate=pl.CostEstimate(flops=6_000_000_000, bytes_accessed=6_000_000, transcendentals=600_000),
    )(roster, arrived, drawn, *blocks, turns)
    return outs[:3], outs[3:]


def local(entity_table, adagrad_state, relations, roster, edge_triples, counts, negatives):
    my_dom = lax.axis_index("dom")
    steps, cap = edge_triples.shape[2], edge_triples.shape[3]
    devices = edge_triples.shape[1]

    edges = jnp.transpose(edge_triples[0], (1, 3, 2, 0)).reshape(steps * 3 * cap, devices)
    packed = jnp.concatenate(
        [edges, counts[0].T, jnp.zeros((LANES - steps * (3 * cap + 1), devices), jnp.int32)], axis=0
    ).T
    arrived = lax.all_to_all(packed, ("bucket", "dom"), split_axis=0, concat_axis=0, tiled=True).T

    rows = entity_table.reshape(2 * SHARD, 2 * HALF).T
    state = adagrad_state.reshape(1, 2 * SHARD)
    held = jnp.concatenate(
        [
            jnp.concatenate([rows[:HALF], rows[HALF:]], axis=1),
            jnp.broadcast_to(jnp.concatenate([state, state], axis=1), (8, LANES)),
        ],
        axis=0,
    )
    column = jnp.arange(PROWS, dtype=jnp.int32)
    roster = roster.reshape(steps, 16)

    def drawn(s):
        negs = place_dom(negatives[s, 0, 0], my_dom)
        return jnp.sum((negs[:, :, None] == column[None, None, :]).astype(jnp.float32), axis=1)

    def turns(s):
        base = s * 3 * cap + cap
        return fetch_turns(table, arrived[base:base + cap])

    arrived, (table,) = tied(arrived, by_rows(relations.T))
    brought, _, arrived = spread(held, bucket_perms(), late=arrived)
    now_turns, now_drawn = turns(0), drawn(0)
    for s in range(steps):
        x, st = select_blocks(brought, roster, s)
        now_drawn, now_turns, gathered = dom_gather(x, now_drawn, now_turns)
        own, other = step_grads(s, roster, arrived, now_drawn, gathered, now_turns)
        more = s + 1 < steps
        parts, now_turns, _ = dom_reduce(own, other, turns(s + 1) if more else None)
        held = adagrad(parts, x, st)
        brought, now_drawn, _ = spread(held, bucket_perms(), drawn(s + 1) if more else None)
    x, st = select_blocks(brought, roster, steps)
    rows = jnp.concatenate([x[:, :64], x[:, 64:]], axis=0).T.reshape(2, SHARD, 2 * HALF)
    return rows, st[0, :64].reshape(2, SHARD)


def solution(mesh):
    in_specs = (
        P("bucket", "dom", None),
        P("bucket", "dom"),
        P(),
        P(),
        P(("bucket", "dom"), None, None, None, None),
        P(("bucket", "dom"), None, None),
        P(None, "bucket", "dom", None, None),
    )
    out_specs = (P("bucket", "dom", None), P("bucket", "dom"))
    return jax.shard_map(local, mesh=mesh, in_specs=in_specs, out_specs=out_specs, check_vma=False)
```

```python
import functools

import jax
import jax.numpy as jnp
from jax import lax
from jax.experimental import pallas as pl
from jax.experimental.pallas import tpu as pltpu
from jax.sharding import PartitionSpec as P

cubic_weight = 0.1
learn_rate = 0.05
epsilon = 1e-06

HALF = 200
LANES = 128
SHARD = 32
PROWS = 512
SLOTS = 1024
MIB = 1024 * 1024

VMEM = pl.BlockSpec(memory_space=pltpu.VMEM)
SMEM = pl.BlockSpec(memory_space=pltpu.SMEM)


def dom_perms():
    def move(fn):
        return [(j, fn(j)) for j in range(16)]

    def shift(j, d):
        return (j // 8) * 8 + (((j // 2) % 4 + d) % 4) * 2 + j % 2

    return dict(
        axis="dom",
        plus=move(lambda j: shift(j, 1)),
        minus=move(lambda j: shift(j, 3)),
        far=move(lambda j: shift(j, 2)),
        flip=move(lambda j: j ^ 8),
        core=move(lambda j: j ^ 1),
    )


def bucket_perms():
    def move(fn):
        return [(w, fn(w)) for w in range(8)]

    return dict(
        axis="bucket",
        plus=move(lambda w: (w + 2) % 8),
        minus=move(lambda w: (w + 6) % 8),
        far=move(lambda w: (w + 4) % 8),
        flip=move(lambda w: w ^ 1),
    )


def tied(value, *extra):
    out = lax.optimization_barrier((value,) + extra)
    return out[0], out[1:]


def spread(block, perms, early=None, late=None):
    def go(v, name):
        return lax.ppermute(v, perms["axis"], perms[name])

    y = go(block, "flip")
    if early is not None:
        y, (early,) = tied(y, early)
    both = jnp.concatenate([block, y], axis=0)
    r, l, f = go(both, "plus"), go(both, "minus"), go(both, "far")
    if late is not None:
        f, (late,) = tied(f, late)
    return [both, r, l, f], early, late


def dom_gather(block, early=None, late=None):
    perms = dom_perms()
    mine, early, late = spread(block, perms, early, late)
    return early, late, mine + [lax.ppermute(v, "dom", perms["core"]) for v in mine]


def dom_reduce(own, other, early=None, late=None):
    perms = dom_perms()

    def go(v, name):
        return lax.ppermute(v, "dom", perms[name])

    swapped = [go(v, "core") for v in other]
    sums = [v + w for v, w in zip(own[1:], swapped[1:])]
    came = [go(v, name) for v, name in zip(sums, ("far", "plus", "minus"))]
    if early is not None:
        came[2], (early,) = tied(came[2], early)
    flipped = (own[0][1] + swapped[0][1]) + ((came[0][1] + came[1][1]) + came[2][1])
    if late is not None:
        flipped, (late,) = tied(flipped, late)
    return (own[0], swapped[0], *came, go(flipped, "flip")), early, late


OUT_PLACE = {0: (0, 0), 1: (0, 1), 6: (1, 0), 7: (1, 1), 4: (2, 0), 5: (2, 1), 2: (3, 0), 3: (3, 1)}


def ring_place(ring):
    return jnp.where(ring == 0, 0, jnp.where(ring == 3, 1, jnp.where(ring == 1, 2, 3)))


def place_dom(rows, me):
    owner = rows >> 5
    ring = ((owner >> 1) - (me >> 1)) & 3
    flip = ((owner >> 3) ^ (me >> 3)) & 1
    core = (owner ^ me) & 1
    return ((core << 3) + (ring_place(ring) << 1) + flip) * SHARD + (rows & (SHARD - 1))


def place_bucket(source, me):
    return (ring_place(((source >> 1) - (me >> 1)) & 3) << 1) + ((source ^ me) & 1)


def lane_index(shape):
    return lax.broadcasted_iota(jnp.int32, shape, 1)


def views(arrays, rows):
    return [(ref, at) for ref in arrays for at in range(0, ref.shape[0], rows)]


def read(ref, at, rows):
    return ref[at:at + rows]


def select_kernel(exchange, steps, roster, *refs):
    blocks, (x_ref, st_ref) = views(refs[:-2], HALF + 8), refs[-2:]
    me = lax.axis_index("bucket")
    lane = lane_index((HALF + 8, LANES))
    picked = []
    for q in range(2):
        wanted = 2 * me + q if exchange == steps else roster[exchange, 2 * me + q]
        at = jnp.int32(0)
        for i in range(16):
            label = i if exchange == 0 else roster[exchange - 1, i]
            at = jnp.where(wanted == label, jnp.int32(i), at)
        place, half = place_bucket(at >> 1, me), at & 1
        got = read(*blocks[0], HALF + 8)
        for p in range(1, 8):
            got = jnp.where(place == p, read(*blocks[p], HALF + 8), got)
        picked.append(jnp.where(half == q, got, pltpu.roll(got, 32 if q else 96, 1)))
    out = jnp.where((lane // SHARD) % 2 == 0, picked[0], picked[1])
    x_ref[...] = out[:HALF]
    st_ref[...] = out[HALF:]


def select_blocks(blocks, roster, exchange):
    return pl.pallas_call(
        functools.partial(select_kernel, exchange, roster.shape[0]),
        out_shape=(
            jax.ShapeDtypeStruct((HALF, LANES), jnp.float32),
            jax.ShapeDtypeStruct((8, LANES), jnp.float32),
        ),
        in_specs=[SMEM] + [VMEM] * len(blocks),
        out_specs=(VMEM, VMEM),
        compiler_params=pltpu.CompilerParams(vmem_limit_bytes=4 * MIB),
        cost_estimate=pl.CostEstimate(flops=200000, bytes_accessed=500000, transcendentals=0),
    )(roster, *blocks)


def adagrad_kernel(own, swapped, far, plus, minus, flipped, x_ref, st_ref, out_ref):
    grad = (own[0] + swapped[0]) + ((far[0] + plus[0]) + (minus[0] + flipped[...]))
    total = jnp.sum(grad * grad, axis=0, keepdims=True)
    total = jnp.broadcast_to(total, (8, LANES))
    total = total + pltpu.roll(total, 64, 1)
    state = st_ref[...] + total / (2.0 * HALF)
    scale = learn_rate / jnp.sqrt(state + epsilon)
    out_ref[:HALF] = x_ref[...] - grad * scale[0:1]
    out_ref[HALF:] = state


def adagrad(parts, x, st):
    return pl.pallas_call(
        adagrad_kernel,
        out_shape=jax.ShapeDtypeStruct((HALF + 8, LANES), jnp.float32),
        in_specs=[VMEM] * 8,
        out_specs=VMEM,
        compiler_params=pltpu.CompilerParams(vmem_limit_bytes=4 * MIB),
        cost_estimate=pl.CostEstimate(flops=200000, bytes_accessed=700000, transcendentals=0),
    )(*parts, x, st)


def split(v):
    high = v.astype(jnp.bfloat16)
    return high, (v - high.astype(jnp.float32)).astype(jnp.bfloat16)


def nn(a, b):
    return lax.dot_general(a, b, (((1,), (0,)), ((), ())), preferred_element_type=jnp.float32)


def nt(a, b):
    return lax.dot_general(a, b, (((1,), (1,)), ((), ())), preferred_element_type=jnp.float32)


def tn(a, b):
    return lax.dot_general(a, b, (((0,), (0,)), ((), ())), preferred_element_type=jnp.float32)


def three(fn, a, b):
    return fn(a[0], b[0]) + (fn(a[0], b[1]) + fn(a[1], b[0]))


def exchange_lanes(tiles):
    lane = lane_index((HALF, LANES))
    low, even = lane < 2 * SHARD, (lane // SHARD) % 2 == 0
    a, b, c, d = tiles
    a, c = jnp.where(low, a, pltpu.roll(c, 64, 1)), jnp.where(low, pltpu.roll(a, 64, 1), c)
    b, d = jnp.where(low, b, pltpu.roll(d, 64, 1)), jnp.where(low, pltpu.roll(b, 64, 1), d)
    a, b = jnp.where(even, a, pltpu.roll(b, 32, 1)), jnp.where(even, pltpu.roll(a, 96, 1), b)
    c, d = jnp.where(even, c, pltpu.roll(d, 32, 1)), jnp.where(even, pltpu.roll(c, 96, 1), d)
    return a, b, c, d


def step_kernel(step, steps, roster, arrived, drawn, *refs):
    arrays, rel, outs, scratch = refs[:-17], refs[-17], refs[-16:-8], refs[-8:]
    blocks = views(arrays, HALF)
    src, dst, sh, sl, dh, dl, th, tl = scratch
    me = lax.axis_index("bucket")
    dom = lax.axis_index("dom")
    base = step * 24

    def row(v):
        return jnp.concatenate([v[i:i + 1] for i in range(8)], axis=1)

    heads = row(place_dom(arrived[base:base + 8] - roster[step, 2 * me] * PROWS, dom))
    tails = row(place_dom(arrived[base + 16:base + 24] - roster[step, 2 * me + 1] * PROWS, dom))
    slot = lax.broadcasted_iota(jnp.int32, (8, LANES), 0)
    live_slot = row(jnp.where(slot < arrived[24 * steps + step:24 * steps + step + 1], 1.0, 0.0))

    quarters = ((src, 0), (dst, 0), (src, HALF), (dst, HALF))
    for t in range(4):
        tiles = exchange_lanes([read(*blocks[4 * t + g], HALF) for g in range(4)])
        for (to, at), tile in zip(quarters, tiles):
            to[at:at + HALF, t * LANES:(t + 1) * LANES] = tile

    sh[...], sl[...] = split(src[...])
    dh[...], dl[...] = split(dst[...])
    th[...], tl[...] = split(dst[...].T)
    count = split(drawn[...])
    mine = lax.broadcasted_iota(jnp.int32, (16, LANES), 0) == lax.broadcasted_iota(jnp.int32, (16, LANES), 1) // 8
    mine = jnp.where(mine, 1.0, 0.0).astype(jnp.bfloat16)
    weight = tn(count[0], mine) + tn(count[1], mine)

    column = lax.broadcasted_iota(jnp.int32, (PROWS, SLOTS), 0)
    head_hot = jnp.where(column == heads, 1.0, 0.0).astype(jnp.bfloat16)
    tail_hot = jnp.where(column == tails, 1.0, 0.0)
    head = nn(sh[...], head_hot) + nn(sl[...], head_hot)
    turn = rel[...].T
    h_re, h_im, r_re, r_im = head[:HALF], head[HALF:], turn[:HALF], turn[HALF:]
    query = split(jnp.concatenate([h_re * r_re - h_im * r_im, h_re * r_im + h_im * r_re], axis=0))
    scores = three(nn, (th[...], tl[...]), query)
    amount = jnp.concatenate([weight] * 8, axis=1) + tail_hot
    scores = jnp.where(amount > 0, scores, -1e30)
    top = jnp.max(scores, axis=0, keepdims=True)
    terms = amount * jnp.exp(scores - top)
    total = jnp.sum(terms, axis=0, keepdims=True)
    adjoint = split(terms * (live_slot / total) - live_slot * tail_hot)
    dst_grad = three(nt, query, adjoint)
    back = three(nn, (dh[...], dl[...]), adjoint)
    b_re, b_im = back[:HALF], back[HALF:]
    to_head = split(jnp.concatenate([b_re * r_re + b_im * r_im, b_im * r_re - b_re * r_im], axis=0))
    src_grad = nt(to_head[0], head_hot) + nt(to_head[1], head_hot)
    flags = jnp.broadcast_to(live_slot, (16, SLOTS)).astype(jnp.bfloat16)
    head_count = nt(flags, head_hot)[0:1]
    tail_count = nt(flags, tail_hot.astype(jnp.bfloat16))[0:1]

    grads = []
    for rows, grad, times in ((src, src_grad, head_count), (dst, dst_grad, tail_count)):
        re, im = rows[:HALF], rows[HALF:]
        modulus = jnp.sqrt(re * re + im * im)
        pull = modulus * ((3.0 * cubic_weight) * times)
        grads.append((grad[:HALF] + pull * re, grad[HALF:] + pull * im))

    for t in range(4):
        at = slice(t * LANES, (t + 1) * LANES)
        tiles = exchange_lanes([grads[0][0][:, at], grads[1][0][:, at], grads[0][1][:, at], grads[1][1][:, at]])
        for g, tile in enumerate(tiles):
            p = 4 * t + g
            array, place = OUT_PLACE[p % 8]
            outs[array + 4 * (p // 8)][place] = tile


def table_kernel(columns, out_ref, came, goes, came_sems, goes_sems):
    depth, out_depth, width = came.shape[0], goes.shape[0], came.shape[2]
    parts = out_ref.shape[0] // width

    def fetch(i):
        at, slot = pl.multiple_of(i * width, width), lax.rem(i, depth)
        return pltpu.make_async_copy(columns.at[:, pl.ds(at, width)], came.at[slot], came_sems.at[slot])

    def store(i):
        at, slot = pl.multiple_of(i * width, width), lax.rem(i, out_depth)
        return pltpu.make_async_copy(goes.at[slot], out_ref.at[pl.ds(at, width), :], goes_sems.at[slot])

    for i in range(depth):
        fetch(jnp.int32(i)).start()

    def part(i, carry):
        fetch(i).wait()

        @pl.when(i >= out_depth)
        def _():
            store(i - out_depth).wait()

        goes[lax.rem(i, out_depth)] = came[lax.rem(i, depth)].T
        store(i).start()

        @pl.when(i + depth < parts)
        def _():
            fetch(i + depth).start()

        return carry

    lax.fori_loop(0, parts, part, 0)
    for i in range(parts - out_depth, parts):
        store(jnp.int32(i)).wait()


def by_rows(columns):
    width, count = columns.shape
    part = 2 * LANES
    return pl.pallas_call(
        table_kernel,
        out_shape=jax.ShapeDtypeStruct((count, width), jnp.float32),
        in_specs=[pl.BlockSpec(memory_space=pl.ANY)],
        out_specs=pl.BlockSpec(memory_space=pl.ANY),
        scratch_shapes=[
            pltpu.VMEM((8, width, part), jnp.float32),
            pltpu.VMEM((4, part, width), jnp.float32),
            pltpu.SemaphoreType.DMA((8,)),
            pltpu.SemaphoreType.DMA((4,)),
        ],
        compiler_params=pltpu.CompilerParams(vmem_limit_bytes=58 * MIB),
        cost_estimate=pl.CostEstimate(flops=0, bytes_accessed=27_000_000, transcendentals=0),
    )(columns)


def turns_kernel(ids, table, out_ref):
    def group(c, carry):
        rows = [table[pl.ds(ids[c // 8, (c % 8) * 16 + u], 1), :] for u in range(16)]
        for u, row in enumerate(rows):
            out_ref[pl.ds(c * 16 + u, 1), :] = row
        return carry

    lax.fori_loop(0, SLOTS // 16, group, 0)


def fetch_turns(table, ids):
    return pl.pallas_call(
        turns_kernel,
        out_shape=jax.ShapeDtypeStruct((SLOTS, table.shape[1]), jnp.float32),
        in_specs=[SMEM, VMEM],
        out_specs=VMEM,
        compiler_params=pltpu.CompilerParams(vmem_limit_bytes=4 * MIB),
        cost_estimate=pl.CostEstimate(flops=0, bytes_accessed=20_000_000, transcendentals=0),
    )(ids, table)


def step_grads(step, roster, arrived, drawn, blocks, turns):
    f32, bf16 = jnp.float32, jnp.bfloat16
    shapes = tuple(jax.ShapeDtypeStruct((n, HALF, LANES), f32) for n in (2, 2, 2, 2))
    outs = pl.pallas_call(
        functools.partial(step_kernel, step, roster.shape[0]),
        out_shape=shapes * 2,
        in_specs=[SMEM] + [VMEM] * (3 + len(blocks)),
        out_specs=(VMEM,) * 8,
        scratch_shapes=[
            pltpu.VMEM((2 * HALF, PROWS), f32),
            pltpu.VMEM((2 * HALF, PROWS), f32),
            pltpu.VMEM((2 * HALF, PROWS), bf16),
            pltpu.VMEM((2 * HALF, PROWS), bf16),
            pltpu.VMEM((2 * HALF, PROWS), bf16),
            pltpu.VMEM((2 * HALF, PROWS), bf16),
            pltpu.VMEM((PROWS, 2 * HALF), bf16),
            pltpu.VMEM((PROWS, 2 * HALF), bf16),
        ],
        compiler_params=pltpu.CompilerParams(vmem_limit_bytes=20 * MIB),
        cost_estimate=pl.CostEstimate(flops=6_000_000_000, bytes_accessed=6_000_000, transcendentals=600_000),
    )(roster, arrived, drawn, *blocks, turns)
    return outs[:4], outs[4:]


def local(entity_table, adagrad_state, relations, roster, edge_triples, counts, negatives):
    my_dom = lax.axis_index("dom")
    steps, cap = edge_triples.shape[2], edge_triples.shape[3]
    devices = edge_triples.shape[1]

    edges = jnp.transpose(edge_triples[0], (1, 3, 2, 0)).reshape(steps * 3 * cap, devices)
    packed = jnp.concatenate(
        [edges, counts[0].T, jnp.zeros((LANES - steps * (3 * cap + 1), devices), jnp.int32)], axis=0
    ).T
    arrived = lax.all_to_all(packed, ("bucket", "dom"), split_axis=0, concat_axis=0, tiled=True).T

    rows = entity_table.reshape(2 * SHARD, 2 * HALF).T
    state = adagrad_state.reshape(1, 2 * SHARD)
    held = jnp.concatenate(
        [
            jnp.concatenate([rows[:HALF], rows[HALF:]], axis=1),
            jnp.broadcast_to(jnp.concatenate([state, state], axis=1), (8, LANES)),
        ],
        axis=0,
    )
    column = jnp.arange(PROWS, dtype=jnp.int32)
    roster = roster.reshape(steps, 16)

    def drawn(s):
        negs = place_dom(negatives[s, 0, 0], my_dom)
        return jnp.sum((negs[:, :, None] == column[None, None, :]).astype(jnp.float32), axis=1)

    def turns(s):
        base = s * 3 * cap + cap
        return fetch_turns(table, arrived[base:base + cap])

    arrived, (table,) = tied(arrived, by_rows(relations.T))
    brought, _, arrived = spread(held, bucket_perms(), late=arrived)
    now_turns, now_drawn = turns(0), drawn(0)
    for s in range(steps):
        x, st = select_blocks(brought, roster, s)
        now_drawn, now_turns, gathered = dom_gather(x, now_drawn, now_turns)
        own, other = step_grads(s, roster, arrived, now_drawn, gathered, now_turns)
        more = s + 1 < steps
        parts, now_turns, _ = dom_reduce(own, other, turns(s + 1) if more else None)
        held = adagrad(parts, x, st)
        brought, now_drawn, _ = spread(held, bucket_perms(), drawn(s + 1) if more else None)
    x, st = select_blocks(brought, roster, steps)
    rows = jnp.concatenate([x[:, :64], x[:, 64:]], axis=0).T.reshape(2, SHARD, 2 * HALF)
    return rows, st[0, :64].reshape(2, SHARD)


def solution(mesh):
    in_specs = (
        P("bucket", "dom", None),
        P("bucket", "dom"),
        P(),
        P(),
        P(("bucket", "dom"), None, None, None, None),
        P(("bucket", "dom"), None, None),
        P(None, "bucket", "dom", None, None),
    )
    out_specs = (P("bucket", "dom", None), P("bucket", "dom"))
    return jax.shard_map(local, mesh=mesh, in_specs=in_specs, out_specs=out_specs, check_vma=False)
```
